32 devices in a mesh: groups: 2 (over y), section: 4 (over z), head: 4 (over x, core).
Axes of the slice: x: 2, y: 2, z: 4, core: 2. Of those that a mesh axis runs over, the one named last changes fastest.
Arguments:
- queries: bfloat16 [1024, 2048], P(('groups', 'section'), 'head'), parts along dimension 0, may hold values from -16 to 16
- token_key_rows: bfloat16 [1024, 1024], P(('groups', 'section'), 'head'), parts along dimension 0, may hold values from -16 to 16
- token_value_rows: bfloat16 [1024, 1024], P(('groups', 'section'), 'head'), parts along dimension 0, may hold values from -6 to 6
- residual: bfloat16 [1024, 5376], P(('groups', 'section', 'head')), parts along dimension 0, may hold values from -6 to 6
- prefix: int32 [8], P('groups'), parts along dimension 0, may hold values from 0 to 128, as said below
- out_weight: bfloat16 [2048, 5376], P('head', 'section'), may hold values from -1 to 1
- post_gain: float32 [5376], replicated, may hold values from 0.25 to 1.75
Outputs:
- layer_out: bfloat16 [1024, 5376], P(('groups', 'section', 'head')), parts along dimension 0
The draws below stay inside these ranges and needn't reach their ends.
There are 2 independent parts, one for each index of `groups`. The reference program is written for one: setup_inputs(seed, part) draws one part's arguments, and reference() takes and returns one part's arrays. A program takes and returns all parts, laid end to end along the dimension named above; an argument that names none is the same for every part. Nothing has to cross between parts.
Inputs may be any that keep to these rules, and one draw needn't show every extreme that they name: `prefix`: some section at index 1 or higher has the most, 128.
All inputs are finite; a program needn't handle non-finite values.
Results may differ from the reference program's by a relative error of at most 0.012.
Values may be sent and summed in bfloat16 or wider, within the bound.
No kernel may reach another device: no remote copies, remote signals or barrier semaphores. Data moves between devices by JAX's collectives and lax.ppermute only.
A program may use at most 64 MiB of HBM per device.

```python
import jax
import jax.numpy as jnp
from jax import lax

D = 5376
HEAD_SIZE = 128
QUERY_HEADS = 16
KEY_VALUE_HEADS = 8
SECTION_ROWS = 128
SEQUENCE_TOKENS = 512
REACH = 1
N_SECTION = 4
N_HEAD = 4


def drawn_pair(key):
    starting_key = jax.random.fold_in(key, 71)
    query_tile_block = jnp.clip(jax.random.normal(jax.random.fold_in(starting_key, 8), (SEQUENCE_TOKENS, QUERY_HEADS * HEAD_SIZE), jnp.float32), -6.0, 6.0)
    key_tile_block = jnp.clip(jax.random.normal(jax.random.fold_in(starting_key, 9), (SEQUENCE_TOKENS, KEY_VALUE_HEADS * HEAD_SIZE), jnp.float32), -6.0, 6.0)
    return (query_tile_block, key_tile_block)


def draw_queries(key, part):
    return drawn_pair(key)[0].astype(jnp.bfloat16)


def draw_token_key_rows(key, part):
    return drawn_pair(key)[1].astype(jnp.bfloat16)


def draw_prefix(key, part):
    section_count = SEQUENCE_TOKENS // SECTION_ROWS
    longest = REACH * SECTION_ROWS
    lengths = jax.random.randint(jax.random.fold_in(key, 301), (section_count,), 0, longest + 1)
    chosen = jax.random.randint(jax.random.fold_in(key, 302), (), REACH, section_count)
    marked = jnp.arange(section_count, dtype=jnp.int32) == chosen
    return jnp.where(marked, longest, lengths).astype(jnp.int32)


def draw_out_weight(key, part):
    fan_in = QUERY_HEADS * HEAD_SIZE
    entries = jnp.clip(jax.random.normal(jax.random.fold_in(key, 403), (fan_in, D), jnp.float32), -6.0, 6.0)
    return (entries * fan_in ** (-0.5)).astype(jnp.bfloat16)


def level_of(key, extent, shards, least, largest):
    gain = 1.0
    for axis_at, blocks in shards:
        heights = jax.random.uniform(jax.random.fold_in(jax.random.fold_in(key, 6), axis_at), (blocks,), jnp.float32, least / len(shards), largest / len(shards))
        gain = gain * jnp.repeat(jnp.exp(heights), extent[axis_at] // blocks).reshape((-1,) + (1,) * (len(extent) - 1 - axis_at))
    return gain


def scatter_about(stream_key, shape, deviation, most, cuts=(), kind=jnp.bfloat16):
    drawn = deviation * jax.random.normal(stream_key, shape, jnp.float32)
    if cuts:
        drawn = drawn * level_of(stream_key, shape, cuts, -0.22, 0.18)
    return jnp.clip(drawn, -most, most).astype(kind)


def setup_inputs(seed: int = 0, part: int = 0) -> dict:
    streams_of = jax.random.split(jax.random.key(seed), 8)
    own_keys = jax.random.split(jax.random.fold_in(streams_of[7], part), 8)
    queries = draw_queries(jax.random.fold_in(jax.random.fold_in(streams_of[7], part), 71), part)
    token_key_rows = draw_token_key_rows(jax.random.fold_in(jax.random.fold_in(streams_of[7], part), 71), part)
    token_value_rows = scatter_about(own_keys[2], (SEQUENCE_TOKENS, KEY_VALUE_HEADS * HEAD_SIZE), 1.0, 6.0, ((0, 4), (1, 4)))
    residual = scatter_about(own_keys[3], (SEQUENCE_TOKENS, D), 1.0, 6.0, ((0, 16),))
    prefix = draw_prefix(jax.random.fold_in(jax.random.fold_in(streams_of[7], part), 71), part)
    out_weight = draw_out_weight(jax.random.fold_in(streams_of[7], 71), part)
    post_gain = jnp.clip(1.0 + 0.15 * jax.random.normal(streams_of[6], (D,), jnp.float32), 0.25, 1.75)
    return dict(queries=queries, token_key_rows=token_key_rows, token_value_rows=token_value_rows, residual=residual, prefix=prefix, out_weight=out_weight, post_gain=post_gain)


score_scale = 168.0 ** (-0.5)
norm_eps = 1e-06

def reference(queries, token_key_rows, token_value_rows, residual, prefix, out_weight, post_gain):
    reachable_blocks = 3 * N_SECTION // 8
    prefix_window_rows = (reachable_blocks + 1) * SECTION_ROWS
    group_width = QUERY_HEADS // KEY_VALUE_HEADS
    head_columns = QUERY_HEADS * HEAD_SIZE // N_HEAD
    extended_keys = jnp.concatenate([jnp.zeros((reachable_blocks * SECTION_ROWS, KEY_VALUE_HEADS * HEAD_SIZE), token_key_rows.dtype), token_key_rows], axis=0)
    extended_values = jnp.concatenate([jnp.zeros((reachable_blocks * SECTION_ROWS, KEY_VALUE_HEADS * HEAD_SIZE), token_value_rows.dtype), token_value_rows], axis=0)

    def one_section(section_at):
        first_row = (section_at * SECTION_ROWS).astype(jnp.int32)
        query_tile_block = lax.dynamic_slice_in_dim(queries, first_row, SECTION_ROWS, 0).astype(jnp.float32)
        query_tile_block = query_tile_block.reshape(SECTION_ROWS, KEY_VALUE_HEADS, group_width, HEAD_SIZE)
        key_tile_block = lax.dynamic_slice_in_dim(extended_keys, first_row, prefix_window_rows, 0).astype(jnp.float32)
        key_tile_block = key_tile_block.reshape(prefix_window_rows, KEY_VALUE_HEADS, HEAD_SIZE)
        value_tile_block = lax.dynamic_slice_in_dim(extended_values, first_row, prefix_window_rows, 0).astype(jnp.float32)
        value_tile_block = value_tile_block.reshape(prefix_window_rows, KEY_VALUE_HEADS, HEAD_SIZE)
        query_pos = first_row + jnp.arange(SECTION_ROWS, dtype=jnp.int32)
        key_pos = first_row - reachable_blocks * SECTION_ROWS + jnp.arange(prefix_window_rows, dtype=jnp.int32)
        seen_tokens = jnp.minimum(first_row, prefix[section_at])
        lower_pos = first_row - seen_tokens
        visible = (key_pos[None, :] <= query_pos[:, None]) & (key_pos[None, :] >= lower_pos)
        scores = jnp.einsum('qkgd,pkd->kgqp', query_tile_block, key_tile_block) * score_scale
        masked = jnp.where(visible, scores, -jnp.inf)
        row_max = lax.optimization_barrier(jnp.max(masked, axis=-1))
        weights = jnp.where(visible, jnp.exp(masked - row_max[..., None]), 0.0)
        denominator = lax.optimization_barrier(jnp.sum(weights, axis=-1))
        weights_low = lax.optimization_barrier(weights.astype(jnp.bfloat16))
        combined = jnp.einsum('kgqp,pkd->qkgd', weights_low.astype(jnp.float32), value_tile_block)
        attention = combined / jnp.transpose(denominator, (2, 0, 1))[..., None]
        attention = attention.reshape(SECTION_ROWS, QUERY_HEADS * HEAD_SIZE).astype(jnp.bfloat16)
        summed = jnp.zeros((SECTION_ROWS, D), jnp.float32)
        for head_at in range(N_HEAD):
            column_block = attention[:, head_at * head_columns:(head_at + 1) * head_columns]
            weight_rows = out_weight[head_at * head_columns:(head_at + 1) * head_columns]
            partial_value = jnp.dot(column_block, weight_rows, preferred_element_type=jnp.float32)
            partial_value = lax.optimization_barrier(partial_value.astype(jnp.bfloat16))
            summed = summed + partial_value.astype(jnp.float32)
        residual_block = lax.dynamic_slice_in_dim(residual, first_row, SECTION_ROWS, 0).astype(jnp.float32)
        mean_square = lax.optimization_barrier(jnp.mean(summed * summed, axis=-1, keepdims=True))
        normed = summed * lax.rsqrt(mean_square + norm_eps) * post_gain.astype(jnp.float32)[None, :]
        return (residual_block + normed).astype(jnp.bfloat16)
    section_outputs = lax.map(one_section, jnp.arange(N_SECTION, dtype=jnp.int32))
    return section_outputs.reshape(SEQUENCE_TOKENS, D)
```

```python
import functools

import jax
import jax.numpy as jnp
from jax import lax
from jax.experimental import pallas as pl
from jax.experimental.pallas import tpu as pltpu
from jax.sharding import PartitionSpec as P

HEAD_SIZE = 128


score_scale = 168.0 ** (-0.5)
floor_value = -1e30
norm_eps = 1e-06
most_paired = 8


def is_paired(count):
    return count & (count - 1) == 0


def shifted(value, axis, steps):
    count = lax.axis_size(axis)
    leading, last = (max(0, -steps), min(count, count - steps))
    return lax.ppermute(value, axis, [(source, source + steps) for source in range(leading, last)])


def exchanged(value, axis, flip):
    count = lax.axis_size(axis)
    return lax.ppermute(value, axis, [(source, source ^ flip) for source in range(count)])


def earlier_sections(own_rows, reach):
    held = own_rows[None]
    stride = 1
    while stride <= reach:
        moved_count = min(stride, reach + 1 - stride)
        held = jnp.concatenate([held, shifted(held[:moved_count], "section", stride)], axis=0)
        stride = stride * 2
    return held[:0:-1].reshape(reach * own_rows.shape[0], own_rows.shape[1])


def attention_kernel(
    reach, prefix_ref, query_ref, key_ref, value_ref, old_key_ref, old_value_ref, out_ref
):
    row_count = query_ref.shape[0]
    key_heads = key_ref.shape[1] // HEAD_SIZE
    group_width = query_ref.shape[1] // (key_heads * HEAD_SIZE)
    section_index = lax.axis_index("section")
    first_row = section_index * row_count
    seen_tokens = jnp.minimum(first_row, prefix_ref[section_index])
    shape = (row_count, (reach + 1) * row_count)
    row = lax.broadcasted_iota(jnp.int32, shape, 0)
    key_pos = lax.broadcasted_iota(jnp.int32, shape, 1) - reach * row_count
    visible = (key_pos <= row) & (key_pos >= -seen_tokens)
    visible = jnp.concatenate([visible] * group_width, axis=0)
    for key_head in range(key_heads):
        columns = slice(key_head * HEAD_SIZE, (key_head + 1) * HEAD_SIZE)
        keys = jnp.concatenate([old_key_ref[:, columns], key_ref[:, columns]], axis=0)
        values = jnp.concatenate([old_value_ref[:, columns], value_ref[:, columns]], axis=0)
        first = key_head * group_width
        stacked = jnp.concatenate(
            [
                query_ref[:, head * HEAD_SIZE : (head + 1) * HEAD_SIZE]
                for head in range(first, first + group_width)
            ],
            axis=0,
        )
        scores = (
            lax.dot_general(
                stacked, keys, (((1,), (1,)), ((), ())), preferred_element_type=jnp.float32
            )
            * score_scale
        )
        masked = jnp.where(visible, scores, floor_value)
        row_max = jnp.max(masked, axis=-1, keepdims=True)
        probs = jnp.where(visible, jnp.exp(masked - row_max), 0.0)
        denominator = jnp.sum(probs, axis=-1, keepdims=True)
        combined = jnp.dot(
            probs.astype(jnp.bfloat16), values, preferred_element_type=jnp.float32
        )
        combined = (combined / denominator).astype(jnp.bfloat16)
        for member in range(group_width):
            head = first + member
            out_ref[:, head * HEAD_SIZE : (head + 1) * HEAD_SIZE] = combined[
                member * row_count : (member + 1) * row_count
            ]


def attend(queries, keys, values, old_keys, old_values, prefix):
    reach = old_keys.shape[0] // keys.shape[0]
    in_vmem = pl.BlockSpec(memory_space=pltpu.VMEM)
    return pl.pallas_call(
        functools.partial(attention_kernel, reach),
        out_shape=jax.ShapeDtypeStruct(queries.shape, jnp.bfloat16),
        in_specs=[pl.BlockSpec(memory_space=pltpu.SMEM)] + [in_vmem] * 5,
        out_specs=in_vmem,
        compiler_params=pltpu.CompilerParams(vmem_limit_bytes=48 * 2**20),
        name="attend",
    )(prefix, queries, keys, values, old_keys, old_values)


def summed_over_heads(partial):
    head_index = lax.axis_index("head")
    flip = 1
    while flip < lax.axis_size("head"):
        count, owners, rows, columns = partial.shape
        pairs = partial.reshape(count, owners // 2, 2, rows, columns)
        bit = (head_index // flip) % 2 == 0
        kept = jnp.where(bit, pairs[:, :, 0], pairs[:, :, 1])
        sent = jnp.where(bit, pairs[:, :, 1], pairs[:, :, 0])
        partial = kept + exchanged(sent.astype(jnp.bfloat16), "head", flip).astype(jnp.float32)
        flip = flip * 2
    return partial[:, 0]


def local(queries, token_key_rows, token_value_rows, residual, prefix, out_weight, post_gain):
    row_count = queries.shape[0]
    own_rows = residual.shape[0]
    section_total = lax.axis_size("section")
    section_index = lax.axis_index("section")
    head_total = lax.axis_size("head")
    reach = 3 * section_total // 8
    old_keys = earlier_sections(token_key_rows, reach)
    old_values = earlier_sections(token_value_rows, reach)
    attention = attend(queries, token_key_rows, token_value_rows, old_keys, old_values, prefix)

    def project(rows):
        product = jnp.dot(rows, out_weight, preferred_element_type=jnp.float32)
        return product.reshape(-1, head_total, own_rows, product.shape[-1])

    if section_total <= most_paired and is_paired(section_total) and is_paired(head_total):
        gathered = [attention]
        for flip in range(1, section_total):
            gathered.append(exchanged(attention, "section", flip))
        own_sums = summed_over_heads(project(jnp.concatenate(gathered, axis=0)))
        pieces = [own_sums[0]]
        for flip in range(1, section_total):
            moved = exchanged(own_sums[flip].astype(jnp.bfloat16), "section", flip)
            pieces.append(moved.astype(jnp.float32))
        flip = 1
        while flip < section_total:
            bit = (section_index // flip) % 2 == 1
            pieces = [
                jnp.where(bit, pieces[place ^ flip], pieces[place])
                for place in range(section_total)
            ]
            flip = flip * 2
        summed = jnp.concatenate(pieces, axis=1)
    else:
        gathered = lax.all_gather(attention, "section", axis=0, tiled=True)
        product = project(gathered).astype(jnp.bfloat16)
        own_sums = lax.psum_scatter(product, "head", scatter_dimension=1, tiled=False)
        pieces = lax.all_to_all(own_sums, "section", 0, 0)
        summed = jnp.transpose(pieces, (1, 0, 2)).reshape(own_rows, -1).astype(jnp.float32)
    mean_square = jnp.mean(summed * summed, axis=-1, keepdims=True)
    normed = summed * lax.rsqrt(mean_square + norm_eps) * post_gain[None, :]
    return (residual.astype(jnp.float32) + normed).astype(jnp.bfloat16)


def solution(mesh):
    placed = (
        P(("groups", "section"), "head"),
        P(("groups", "section"), "head"),
        P(("groups", "section"), "head"),
        P(("groups", "section", "head"), None),
        P("groups"),
        P("head", "section"),
        P(),
    )
    return jax.shard_map(
        local,
        mesh=mesh,
        in_specs=placed,
        out_specs=P(("groups", "section", "head"), None),
        check_vma=False,
    )
```

```python
import functools

import jax
import jax.numpy as jnp
from jax import lax
from jax.experimental import pallas as pl
from jax.experimental.pallas import tpu as pltpu
from jax.sharding import PartitionSpec as P

HEAD_SIZE = 128


score_scale = 168.0 ** (-0.5)
floor_value = -1e30
norm_eps = 1e-06
vmem_bytes = 48 * 2**20
most_paired = 8

in_vmem = pl.BlockSpec(memory_space=pltpu.VMEM)
in_smem = pl.BlockSpec(memory_space=pltpu.SMEM)
anywhere = pl.BlockSpec(memory_space=pl.ANY)


def is_power(count):
    return count & (count - 1) == 0


def rotated(value, axis, steps):
    count = lax.axis_size(axis)
    return lax.ppermute(value, axis, [(at, (at + steps) % count) for at in range(count)])


def exchanged(value, axis, flip):
    count = lax.axis_size(axis)
    return lax.ppermute(value, axis, [(at, at ^ flip) for at in range(count)])


def earlier_sections(own_rows, reach):
    held = own_rows[None]
    stride = 1
    while stride <= reach:
        moved_count = min(stride, reach + 1 - stride)
        held = jnp.concatenate([held, rotated(held[:moved_count], "section", stride)], axis=0)
        stride = stride * 2
    return held[:0:-1].reshape(reach * own_rows.shape[0], own_rows.shape[1])


def head_columns(head):
    return slice(head * HEAD_SIZE, (head + 1) * HEAD_SIZE)


def stacked_queries(query_ref, key_head, group_width):
    first = key_head * group_width
    return jnp.concatenate(
        [query_ref[:, head_columns(head)] for head in range(first, first + group_width)], axis=0
    )


def scaled_scores(queries, keys):
    product = lax.dot_general(
        queries, keys, (((1,), (1,)), ((), ())), preferred_element_type=jnp.float32
    )
    return product * score_scale


def own_kernel(
    prefix_ref, query_in, key_in, value_in, query_ref, value_ref, score_ref, bias_ref, key_ref, sems
):
    copies = [
        pltpu.make_async_copy(query_in, query_ref, sems.at[0]),
        pltpu.make_async_copy(key_in, key_ref, sems.at[1]),
        pltpu.make_async_copy(value_in, value_ref, sems.at[2]),
    ]
    for copy in copies:
        copy.start()
    row_count = query_ref.shape[0]
    key_heads = key_ref.shape[1] // HEAD_SIZE
    group_width = query_ref.shape[1] // (key_heads * HEAD_SIZE)
    section_index = lax.axis_index("section")
    seen_tokens = jnp.minimum(section_index * row_count, prefix_ref[section_index])
    old_pos = lax.broadcasted_iota(jnp.int32, bias_ref.shape, 1) - bias_ref.shape[1]
    bias_ref[...] = jnp.where(old_pos >= -seen_tokens, 0.0, floor_value)
    shape = (row_count, row_count)
    visible = lax.broadcasted_iota(jnp.int32, shape, 1) <= lax.broadcasted_iota(jnp.int32, shape, 0)
    visible = jnp.concatenate([visible] * group_width, axis=0)
    for copy in copies:
        copy.wait()
    for key_head in range(key_heads):
        queries = stacked_queries(query_ref, key_head, group_width)
        scores = scaled_scores(queries, key_ref[:, head_columns(key_head)])
        score_ref[key_head] = jnp.where(visible, scores, floor_value)


def rest_kernel(
    query_ref, value_ref, score_ref, bias_ref, old_key_ref, old_value_ref, out_ref
):
    row_count = query_ref.shape[0]
    key_heads = value_ref.shape[1] // HEAD_SIZE
    group_width = query_ref.shape[1] // (key_heads * HEAD_SIZE)
    bias = jnp.concatenate([bias_ref[...]] * group_width, axis=0)
    for key_head in range(key_heads):
        columns = head_columns(key_head)
        queries = stacked_queries(query_ref, key_head, group_width)
        old_scores = scaled_scores(queries, old_key_ref[:, columns]) + bias
        masked = jnp.concatenate([old_scores, score_ref[key_head]], axis=1)
        row_max = jnp.max(masked, axis=-1, keepdims=True)
        probs = jnp.exp(masked - row_max)
        denominator = jnp.sum(probs, axis=-1, keepdims=True)
        values = jnp.concatenate([old_value_ref[:, columns], value_ref[:, columns]], axis=0)
        combined = jnp.dot(
            probs.astype(jnp.bfloat16), values, preferred_element_type=jnp.float32
        )
        combined = (combined / denominator).astype(jnp.bfloat16)
        for member in range(group_width):
            rows = slice(member * row_count, (member + 1) * row_count)
            out_ref[:, head_columns(key_head * group_width + member)] = combined[rows]


def attend(queries, keys, values, prefix, reach):
    row_count = queries.shape[0]
    key_heads = keys.shape[1] // HEAD_SIZE
    stacked_rows = queries.shape[1] // (key_heads * HEAD_SIZE) * row_count
    params = pltpu.CompilerParams(vmem_limit_bytes=vmem_bytes)
    old_keys = earlier_sections(keys, reach)
    old_values = earlier_sections(values, reach)
    own = pl.pallas_call(
        own_kernel,
        out_shape=(
            jax.ShapeDtypeStruct(queries.shape, queries.dtype),
            jax.ShapeDtypeStruct(values.shape, values.dtype),
            jax.ShapeDtypeStruct((key_heads, stacked_rows, row_count), jnp.float32),
            jax.ShapeDtypeStruct((row_count, reach * row_count), jnp.float32),
        ),
        in_specs=[in_smem, anywhere, anywhere, anywhere],
        out_specs=(in_vmem,) * 4,
        scratch_shapes=[pltpu.VMEM(keys.shape, keys.dtype), pltpu.SemaphoreType.DMA((3,))],
        compiler_params=params,
        name="own_scores",
    )(prefix, queries, keys, values)
    return pl.pallas_call(
        rest_kernel,
        out_shape=jax.ShapeDtypeStruct(queries.shape, jnp.bfloat16),
        in_specs=[in_vmem] * 6,
        out_specs=in_vmem,
        compiler_params=params,
        name="attend",
    )(*own, old_keys, old_values)


def flips_in_order(count):
    bits = count.bit_length() - 1
    turned = [sum((at >> bit & 1) << (bits - 1 - bit) for bit in range(bits)) for at in range(count)]
    return sorted(range(count), key=lambda at: -turned[at])


def project_kernel(head_total, *refs):
    *row_refs, weight_ref, sent_ref, kept_ref = refs
    own_rows = row_refs[0].shape[0] // head_total
    head_index = lax.axis_index("head")
    blocks = []
    for row_ref in row_refs:
        for flip in flips_in_order(head_total):
            first = pl.multiple_of((head_index ^ flip) * own_rows, own_rows)
            blocks.append(row_ref[pl.ds(first, own_rows), :])
    product = lax.dot_general(
        jnp.concatenate(blocks, axis=0),
        weight_ref[...],
        (((1,), (1,)), ((), ())),
        preferred_element_type=jnp.float32,
    )
    half = sent_ref.shape[1]
    for at in range(len(row_refs)):
        first = 2 * half * at
        sent_ref[at] = product[first : first + half].astype(jnp.bfloat16)
        kept_ref[at] = product[first + half : first + 2 * half]


def project(chunks, turned_weight, head_total):
    shape = (len(chunks), chunks[0].shape[0] // 2, turned_weight.shape[0])
    return pl.pallas_call(
        functools.partial(project_kernel, head_total),
        out_shape=(
            jax.ShapeDtypeStruct(shape, jnp.bfloat16),
            jax.ShapeDtypeStruct(shape, jnp.float32),
        ),
        in_specs=[in_vmem] * (len(chunks) + 1),
        out_specs=(in_vmem, in_vmem),
        compiler_params=pltpu.CompilerParams(vmem_limit_bytes=vmem_bytes),
        name="project",
    )(*chunks, turned_weight)


def head_sums(chunks, turned_weight):
    head_total = lax.axis_size("head")
    sent, kept = project(chunks, turned_weight, head_total)
    flip = 1
    while True:
        total = kept + exchanged(sent, "head", flip).astype(jnp.float32)
        flip = flip * 2
        if flip == head_total:
            return total
        half = total.shape[1] // 2
        sent, kept = total[:, :half].astype(jnp.bfloat16), total[:, half:]


def norm_kernel(own_ref, *refs):
    *moved_refs, residual_ref, gain_ref, out_ref, piece_ref = refs
    section_total, _, width = piece_ref.shape
    columns = section_total * width
    piece_ref[0] = own_ref[...]
    square = jnp.sum(piece_ref[0] * piece_ref[0], axis=-1, keepdims=True)
    for at, moved_ref in enumerate(moved_refs):
        piece = moved_ref[...].astype(jnp.float32)
        piece_ref[at + 1] = piece
        square += jnp.sum(piece * piece, axis=-1, keepdims=True)
    scale = lax.rsqrt(square / columns + norm_eps)
    section_index = lax.axis_index("section")
    for at in range(section_total):
        place = slice(at * width, (at + 1) * width)
        normed = piece_ref[section_index ^ at] * scale * gain_ref[:, place]
        out_ref[:, place] = (residual_ref[:, place].astype(jnp.float32) + normed).astype(jnp.bfloat16)


def norm(pieces, residual, post_gain):
    return pl.pallas_call(
        norm_kernel,
        out_shape=jax.ShapeDtypeStruct(residual.shape, jnp.bfloat16),
        in_specs=[in_vmem] * (len(pieces) + 2),
        out_specs=in_vmem,
        scratch_shapes=[pltpu.VMEM((len(pieces), *pieces[0].shape), jnp.float32)],
        compiler_params=pltpu.CompilerParams(vmem_limit_bytes=vmem_bytes),
        name="norm",
    )(*pieces, residual, post_gain[None, :])


def local(queries, token_key_rows, token_value_rows, residual, prefix, out_weight, post_gain):
    own_rows = residual.shape[0]
    section_total = lax.axis_size("section")
    head_total = lax.axis_size("head")
    reach = 3 * section_total // 8
    attention = attend(queries, token_key_rows, token_value_rows, prefix, reach)
    if section_total <= most_paired and is_power(section_total) and is_power(head_total):
        turned_weight = out_weight.T
        flips = list(range(section_total - 1, 0, -1))
        gathered = {flip: exchanged(attention, "section", flip) for flip in flips}
        gathered[0] = attention
        pieces = [None] * section_total
        for flip in [0, *flips]:
            total = head_sums([gathered[flip]], turned_weight)[0]
            if flip:
                total = exchanged(total.astype(jnp.bfloat16), "section", flip)
            pieces[flip] = total
        return norm(pieces, residual, post_gain)
    gathered = lax.all_gather(attention, "section", axis=0, tiled=True)
    product = jnp.dot(gathered, out_weight, preferred_element_type=jnp.float32)
    product = product.astype(jnp.bfloat16).reshape(-1, head_total, own_rows, product.shape[-1])
    sums = lax.psum_scatter(product, "head", scatter_dimension=1, tiled=False)
    pieces = lax.all_to_all(sums, "section", 0, 0)
    summed = jnp.transpose(pieces, (1, 0, 2)).reshape(own_rows, -1).astype(jnp.float32)
    mean_square = jnp.mean(summed * summed, axis=-1, keepdims=True)
    normed = summed * lax.rsqrt(mean_square + norm_eps) * post_gain[None, :]
    return (residual.astype(jnp.float32) + normed).astype(jnp.bfloat16)


def solution(mesh):
    placed = (
        P(("groups", "section"), "head"),
        P(("groups", "section"), "head"),
        P(("groups", "section"), "head"),
        P(("groups", "section", "head"), None),
        P("groups"),
        P("head", "section"),
        P(),
    )
    return jax.shard_map(
        local,
        mesh=mesh,
        in_specs=placed,
        out_specs=P(("groups", "section", "head"), None),
        check_vma=False,
    )
```

```python
import functools

import jax
import jax.numpy as jnp
from jax import lax
from jax.experimental import pallas as pl
from jax.experimental.pallas import tpu as pltpu
from jax.sharding import PartitionSpec as P

HEAD_SIZE = 128


score_scale = 168.0 ** (-0.5)
floor_value = -1e30
norm_eps = 1e-06
vmem_bytes = 24 * 2**20
most_paired = 8

in_vmem = pl.BlockSpec(memory_space=pltpu.VMEM)
in_smem = pl.BlockSpec(memory_space=pltpu.SMEM)
in_hbm = pl.BlockSpec(memory_space=pltpu.HBM)
anywhere = pl.BlockSpec(memory_space=pl.ANY)


no_cost = pl.CostEstimate(flops=0, transcendentals=0, bytes_accessed=0)
project_cost = pl.CostEstimate(flops=3 * 10**9, transcendentals=0, bytes_accessed=0)


def is_power(count):
    return count & (count - 1) == 0


def rotated(value, axis, steps):
    count = lax.axis_size(axis)
    return lax.ppermute(value, axis, [(at, (at + steps) % count) for at in range(count)])


def exchanged(value, axis, flip):
    count = lax.axis_size(axis)
    return lax.ppermute(value, axis, [(at, at ^ flip) for at in range(count)])


def earlier_sections(own_rows, reach):
    held = own_rows[None]
    stride = 1
    while stride <= reach:
        moved_count = min(stride, reach + 1 - stride)
        held = jnp.concatenate([held, rotated(held[:moved_count], "section", stride)], axis=0)
        stride = stride * 2
    return held[:0:-1].reshape(reach * own_rows.shape[0], own_rows.shape[1])


def head_columns(head):
    return slice(head * HEAD_SIZE, (head + 1) * HEAD_SIZE)


def stacked_queries(query_ref, key_head, group_width):
    first = key_head * group_width
    return jnp.concatenate(
        [query_ref[:, head_columns(head)] for head in range(first, first + group_width)], axis=0
    )


def scaled_scores(queries, keys):
    product = lax.dot_general(
        queries, keys, (((1,), (1,)), ((), ())), preferred_element_type=jnp.float32
    )
    return product * score_scale


def own_kernel(
    prefix_in,
    query_in,
    key_in,
    value_in,
    weight_in,
    query_ref,
    value_ref,
    weight_ref,
    score_ref,
    bias_ref,
    key_ref,
    prefix_ref,
    sems,
):
    loads = [
        pltpu.make_async_copy(source, target, sems.at[at])
        for at, (source, target) in enumerate(
            (
                (prefix_in, prefix_ref),
                (query_in, query_ref),
                (key_in, key_ref),
                (value_in, value_ref),
                (weight_in, weight_ref),
            )
        )
    ]
    for load in loads:
        load.start()
    row_count = query_ref.shape[0]
    key_heads = key_ref.shape[1] // HEAD_SIZE
    group_width = query_ref.shape[1] // (key_heads * HEAD_SIZE)
    shape = (row_count, row_count)
    visible = lax.broadcasted_iota(jnp.int32, shape, 1) <= lax.broadcasted_iota(jnp.int32, shape, 0)
    visible = jnp.concatenate([visible] * group_width, axis=0)
    for load in loads[:3]:
        load.wait()
    section_index = lax.axis_index("section")
    seen_tokens = jnp.minimum(section_index * row_count, prefix_ref[section_index])
    old_pos = lax.broadcasted_iota(jnp.int32, bias_ref.shape, 1) - bias_ref.shape[1]
    bias_ref[...] = jnp.where(old_pos >= -seen_tokens, 0.0, floor_value)
    for key_head in range(key_heads):
        queries = stacked_queries(query_ref, key_head, group_width)
        scores = scaled_scores(queries, key_ref[:, head_columns(key_head)])
        score_ref[key_head] = jnp.where(visible, scores, floor_value)
    for load in loads[3:]:
        load.wait()


def rest_kernel(
    query_ref, value_ref, score_ref, bias_ref, old_key_ref, old_value_ref, out_ref
):
    row_count = query_ref.shape[0]
    key_heads = value_ref.shape[1] // HEAD_SIZE
    group_width = query_ref.shape[1] // (key_heads * HEAD_SIZE)
    bias = jnp.concatenate([bias_ref[...]] * group_width, axis=0)
    for key_head in range(key_heads):
        columns = head_columns(key_head)
        queries = stacked_queries(query_ref, key_head, group_width)
        old_scores = scaled_scores(queries, old_key_ref[:, columns]) + bias
        masked = jnp.concatenate([old_scores, score_ref[key_head]], axis=1)
        row_max = jnp.max(masked, axis=-1, keepdims=True)
        probs = jnp.exp(masked - row_max)
        denominator = jnp.sum(probs, axis=-1, keepdims=True)
        values = jnp.concatenate([old_value_ref[:, columns], value_ref[:, columns]], axis=0)
        combined = jnp.dot(
            probs.astype(jnp.bfloat16), values, preferred_element_type=jnp.float32
        )
        combined = (combined / denominator).astype(jnp.bfloat16)
        for member in range(group_width):
            rows = slice(member * row_count, (member + 1) * row_count)
            out_ref[:, head_columns(key_head * group_width + member)] = combined[rows]


def attend(queries, keys, values, prefix, turned_weight, reach):
    row_count = queries.shape[0]
    key_heads = keys.shape[1] // HEAD_SIZE
    stacked_rows = queries.shape[1] // (key_heads * HEAD_SIZE) * row_count
    params = pltpu.CompilerParams(vmem_limit_bytes=vmem_bytes)
    old_keys = earlier_sections(keys, reach)
    old_values = earlier_sections(values, reach)
    like = lambda array: jax.ShapeDtypeStruct(array.shape, array.dtype)
    own_queries, own_values, weight, scores, bias = pl.pallas_call(
        own_kernel,
        out_shape=(
            like(queries),
            like(values),
            like(turned_weight),
            jax.ShapeDtypeStruct((key_heads, stacked_rows, row_count), jnp.float32),
            jax.ShapeDtypeStruct((row_count, reach * row_count), jnp.float32),
        ),
        in_specs=[in_hbm] * 5,
        out_specs=(in_vmem,) * 5,
        scratch_shapes=[
            pltpu.VMEM(keys.shape, keys.dtype),
            pltpu.SMEM(prefix.shape, prefix.dtype),
            pltpu.SemaphoreType.DMA((5,)),
        ],
        compiler_params=params,
        cost_estimate=no_cost,
        name="own_scores",
    )(*(pltpu.with_memory_space_constraint(array, pltpu.HBM) for array in (prefix, queries, keys, values, turned_weight)))
    attention = pl.pallas_call(
        rest_kernel,
        out_shape=like(queries),
        in_specs=[in_vmem] * 6,
        out_specs=in_vmem,
        compiler_params=params,
        cost_estimate=no_cost,
        name="attend",
    )(own_queries, own_values, scores, bias, old_keys, old_values)
    return attention, weight


def flips_in_order(count):
    bits = count.bit_length() - 1
    turned = [sum((at >> bit & 1) << (bits - 1 - bit) for bit in range(bits)) for at in range(count)]
    return sorted(range(count), key=lambda at: -turned[at])


def project_kernel(head_total, chunk_count, *refs):
    row_refs, weight_ref = refs[:chunk_count], refs[chunk_count]
    sent_ref, kept_ref = refs[-2:]
    own_rows = row_refs[0].shape[0] // head_total
    head_index = lax.axis_index("head")
    blocks = []
    for row_ref in row_refs:
        for flip in flips_in_order(head_total):
            first = pl.multiple_of((head_index ^ flip) * own_rows, own_rows)
            blocks.append(row_ref[pl.ds(first, own_rows), :])
    product = lax.dot_general(
        jnp.concatenate(blocks, axis=0),
        weight_ref[...],
        (((1,), (1,)), ((), ())),
        preferred_element_type=jnp.float32,
    )
    half = sent_ref.shape[1]
    for at in range(chunk_count):
        first = 2 * half * at
        sent_ref[at] = product[first : first + half].astype(jnp.bfloat16)
        kept_ref[at] = product[first + half : first + 2 * half]


def project(chunks, turned_weight, head_total, earlier):
    shape = (len(chunks), chunks[0].shape[0] // 2, turned_weight.shape[0])
    return pl.pallas_call(
        functools.partial(project_kernel, head_total, len(chunks)),
        out_shape=(
            jax.ShapeDtypeStruct(shape, jnp.bfloat16),
            jax.ShapeDtypeStruct(shape, jnp.float32),
        ),
        in_specs=[in_vmem] * (len(chunks) + 1) + [anywhere] * len(earlier),
        out_specs=(in_vmem, in_vmem),
        compiler_params=pltpu.CompilerParams(vmem_limit_bytes=vmem_bytes),
        cost_estimate=project_cost,
        name="project",
    )(*chunks, turned_weight, *earlier)


def fold_kernel(kept_ref, arrived_ref, sent_ref, half_ref):
    total = kept_ref[...] + arrived_ref[...].astype(jnp.float32)
    half = half_ref.shape[1]
    sent_ref[...] = total[:, :half].astype(jnp.bfloat16)
    half_ref[...] = total[:, half:]


def fold(kept, arrived):
    chunks, rows, columns = kept.shape
    half = (chunks, rows // 2, columns)
    return pl.pallas_call(
        fold_kernel,
        out_shape=(
            jax.ShapeDtypeStruct(half, jnp.bfloat16),
            jax.ShapeDtypeStruct(half, jnp.float32),
        ),
        in_specs=[in_vmem] * 2,
        out_specs=(in_vmem,) * 2,
        compiler_params=pltpu.CompilerParams(vmem_limit_bytes=vmem_bytes),
        cost_estimate=no_cost,
        name="fold",
    )(kept, arrived)


def core_exchanged(array, one):
    return lax.fori_loop(0, one, lambda _, array: exchanged(array, "head", 1), array)


def squares_kernel(has_earlier, *refs):
    *piece_refs, out_ref = refs
    total = piece_refs.pop()[:, :1] if has_earlier else 0.0
    for piece_ref in piece_refs:
        piece = piece_ref[...].astype(jnp.float32)
        total = total + jnp.sum(piece * piece, axis=-1, keepdims=True)
    out_ref[...] = jnp.broadcast_to(total, out_ref.shape)


def squares(pieces, earlier):
    given = list(pieces) if earlier is None else [*pieces, earlier]
    return pl.pallas_call(
        functools.partial(squares_kernel, earlier is not None),
        out_shape=jax.ShapeDtypeStruct((pieces[0].shape[0], HEAD_SIZE), jnp.float32),
        in_specs=[in_vmem] * len(given),
        out_specs=in_vmem,
        compiler_params=pltpu.CompilerParams(vmem_limit_bytes=vmem_bytes),
        cost_estimate=no_cost,
        name="squares",
    )(*given)


def norm_kernel(count, *refs):
    piece_refs = refs[:count]
    squares_ref, residual_ref, gain_ref, out_ref, piece_ref = refs[count:]
    width = piece_ref.shape[2]
    for at, moved_ref in enumerate(piece_refs):
        piece_ref[at] = moved_ref[...].astype(jnp.float32)
    last = piece_ref[last_flip(count)]
    square = squares_ref[:, :1] + jnp.sum(last * last, axis=-1, keepdims=True)
    scale = lax.rsqrt(square / (count * width) + norm_eps)
    section_index = lax.axis_index("section")
    for at in range(count):
        place = slice(at * width, (at + 1) * width)
        normed = piece_ref[section_index ^ at] * scale * gain_ref[:, place]
        out_ref[:, place] = (residual_ref[:, place].astype(jnp.float32) + normed).astype(jnp.bfloat16)


def last_flip(section_total):
    return section_flips(section_total)[-1][-1]


def section_flips(section_total):
    return [[0, 1]] + [[flip] for flip in range(section_total - 1, 1, -1)]


def norm(pieces, residual, post_gain):
    early = None
    for group in section_flips(len(pieces))[:-1]:
        early = squares([pieces[flip] for flip in group], early)
    return pl.pallas_call(
        functools.partial(norm_kernel, len(pieces)),
        out_shape=jax.ShapeDtypeStruct(residual.shape, jnp.bfloat16),
        in_specs=[in_vmem] * (len(pieces) + 3),
        out_specs=in_vmem,
        scratch_shapes=[pltpu.VMEM((len(pieces), *pieces[0].shape), jnp.float32)],
        compiler_params=pltpu.CompilerParams(vmem_limit_bytes=vmem_bytes),
        cost_estimate=no_cost,
        name="norm",
    )(*pieces, early, residual, post_gain[None, :])


def local(queries, token_key_rows, token_value_rows, residual, prefix, out_weight, post_gain):
    own_rows = residual.shape[0]
    section_total = lax.axis_size("section")
    head_total = lax.axis_size("head")
    reach = 3 * section_total // 8
    attention, turned_weight = attend(
        queries, token_key_rows, token_value_rows, prefix, out_weight.T, reach
    )
    if 2 < section_total <= most_paired and is_power(section_total) and head_total == 4:
        groups = section_flips(section_total)
        gathered = {0: attention}
        for group in groups:
            for flip in group:
                if flip:
                    gathered[flip] = exchanged(attention, "section", flip)
        one = jnp.minimum((prefix[0] & 7) + 1, 1)
        pieces = [None] * section_total
        sent, halves, arrivals = None, [], []
        for group in groups:
            chunks = [gathered[flip] for flip in group]
            sent, kept = project(chunks, turned_weight, head_total, [] if sent is None else [sent])
            arrived = core_exchanged(sent, one)
            sent, half = fold(kept, arrived)
            halves.append(half)
            arrivals.append(exchanged(sent, "head", 2))
        for group, half, arrived in zip(groups, halves, arrivals, strict=True):
            for at, flip in enumerate(group):
                total = half[at] + arrived[at].astype(jnp.float32)
                if flip:
                    total = exchanged(total.astype(jnp.bfloat16), "section", flip)
                pieces[flip] = total
        return norm(pieces, residual, post_gain)
    gathered = lax.all_gather(attention, "section", axis=0, tiled=True)
    product = jnp.dot(gathered, turned_weight.T, preferred_element_type=jnp.float32)
    product = product.astype(jnp.bfloat16).reshape(-1, head_total, own_rows, product.shape[-1])
    sums = lax.psum_scatter(product, "head", scatter_dimension=1, tiled=False)
    pieces = lax.all_to_all(sums, "section", 0, 0)
    summed = jnp.transpose(pieces, (1, 0, 2)).reshape(own_rows, -1).astype(jnp.float32)
    mean_square = jnp.mean(summed * summed, axis=-1, keepdims=True)
    normed = summed * lax.rsqrt(mean_square + norm_eps) * post_gain[None, :]
    return (residual.astype(jnp.float32) + normed).astype(jnp.bfloat16)


def solution(mesh):
    placed = (
        P(("groups", "section"), "head"),
        P(("groups", "section"), "head"),
        P(("groups", "section"), "head"),
        P(("groups", "section", "head"), None),
        P("groups"),
        P("head", "section"),
        P(),
    )
    return jax.shard_map(
        local,
        mesh=mesh,
        in_specs=placed,
        out_specs=P(("groups", "section", "head"), None),
        check_vma=False,
    )
```

```python
import functools

import jax
import jax.numpy as jnp
from jax import lax
from jax.experimental import pallas as pl
from jax.experimental.pallas import tpu as pltpu
from jax.sharding import PartitionSpec as P

HEAD_SIZE = 128


score_scale = 168.0 ** (-0.5)
floor_value = -1e30
norm_eps = 1e-06
vmem_bytes = 24 * 2**20
owner_flips = ((3, 1), (2, 0))
most_paired = 8

in_vmem = pl.BlockSpec(memory_space=pltpu.VMEM)
in_smem = pl.BlockSpec(memory_space=pltpu.SMEM)
in_hbm = pl.BlockSpec(memory_space=pltpu.HBM)
anywhere = pl.BlockSpec(memory_space=pl.ANY)


no_cost = pl.CostEstimate(flops=0, transcendentals=0, bytes_accessed=0)
project_cost = pl.CostEstimate(flops=3 * 10**9, transcendentals=0, bytes_accessed=0)


def is_power(count):
    return count & (count - 1) == 0


def rotated(value, axis, steps):
    count = lax.axis_size(axis)
    return lax.ppermute(value, axis, [(at, (at + steps) % count) for at in range(count)])


def exchanged(value, axis, flip):
    count = lax.axis_size(axis)
    return lax.ppermute(value, axis, [(at, at ^ flip) for at in range(count)])


def earlier_sections(own_rows, reach):
    held = own_rows[None]
    stride = 1
    while stride <= reach:
        moved_count = min(stride, reach + 1 - stride)
        held = jnp.concatenate([held, rotated(held[:moved_count], "section", stride)], axis=0)
        stride = stride * 2
    return held[:0:-1].reshape(reach * own_rows.shape[0], own_rows.shape[1])


def head_columns(head):
    return slice(head * HEAD_SIZE, (head + 1) * HEAD_SIZE)


def stacked_queries(query_ref, key_head, group_width):
    first = key_head * group_width
    return jnp.concatenate(
        [query_ref[:, head_columns(head)] for head in range(first, first + group_width)], axis=0
    )


def scaled_scores(queries, keys):
    product = lax.dot_general(
        queries, keys, (((1,), (1,)), ((), ())), preferred_element_type=jnp.float32
    )
    return product * score_scale


def own_kernel(
    prefix_in,
    query_in,
    key_in,
    value_in,
    weight_in,
    query_ref,
    value_ref,
    weight_ref,
    score_ref,
    bias_ref,
    key_ref,
    prefix_ref,
    sems,
):
    loads = [
        pltpu.make_async_copy(source, target, sems.at[at])
        for at, (source, target) in enumerate(
            (
                (prefix_in, prefix_ref),
                (query_in, query_ref),
                (key_in, key_ref),
                (value_in, value_ref),
                (weight_in, weight_ref),
            )
        )
    ]
    for load in loads:
        load.start()
    row_count = query_ref.shape[0]
    key_heads = key_ref.shape[1] // HEAD_SIZE
    group_width = query_ref.shape[1] // (key_heads * HEAD_SIZE)
    shape = (row_count, row_count)
    visible = lax.broadcasted_iota(jnp.int32, shape, 1) <= lax.broadcasted_iota(jnp.int32, shape, 0)
    visible = jnp.concatenate([visible] * group_width, axis=0)
    for load in loads[:3]:
        load.wait()
    section_index = lax.axis_index("section")
    seen_tokens = jnp.minimum(section_index * row_count, prefix_ref[section_index])
    old_pos = lax.broadcasted_iota(jnp.int32, bias_ref.shape, 1) - bias_ref.shape[1]
    bias_ref[...] = jnp.where(old_pos >= -seen_tokens, 0.0, floor_value)
    for key_head in range(key_heads):
        queries = stacked_queries(query_ref, key_head, group_width)
        scores = scaled_scores(queries, key_ref[:, head_columns(key_head)])
        score_ref[key_head] = jnp.where(visible, scores, floor_value)
    for load in loads[3:]:
        load.wait()


def rest_kernel(
    query_ref,
    value_ref,
    score_ref,
    bias_ref,
    old_key_ref,
    old_value_ref,
    *out_refs,
):
    row_count = query_ref.shape[0]
    key_heads = value_ref.shape[1] // HEAD_SIZE
    group_width = query_ref.shape[1] // (key_heads * HEAD_SIZE)
    whole_ref = out_refs[-1]
    bias = jnp.concatenate([bias_ref[...]] * group_width, axis=0)
    for key_head in range(key_heads):
        columns = head_columns(key_head)
        queries = stacked_queries(query_ref, key_head, group_width)
        old_scores = scaled_scores(queries, old_key_ref[:, columns]) + bias
        masked = jnp.concatenate([old_scores, score_ref[key_head]], axis=1)
        row_max = jnp.max(masked, axis=-1, keepdims=True)
        probs = jnp.exp(masked - row_max)
        denominator = jnp.sum(probs, axis=-1, keepdims=True)
        values = jnp.concatenate([old_value_ref[:, columns], value_ref[:, columns]], axis=0)
        combined = jnp.dot(
            probs.astype(jnp.bfloat16), values, preferred_element_type=jnp.float32
        )
        combined = (combined / denominator).astype(jnp.bfloat16)
        for member in range(group_width):
            rows = slice(member * row_count, (member + 1) * row_count)
            whole_ref[:, head_columns(key_head * group_width + member)] = combined[rows]
    if len(out_refs) > 1:
        head_index = lax.axis_index("head")
        for out_ref, flips in zip(out_refs[:2], owner_flips, strict=True):
            own_rows = out_ref.shape[0] // len(flips)
            for at, flip in enumerate(flips):
                first = pl.multiple_of((head_index ^ flip) * own_rows, own_rows)
                out_ref[at * own_rows : (at + 1) * own_rows] = whole_ref[pl.ds(first, own_rows), :]


def attend(queries, keys, values, prefix, turned_weight, reach, in_halves):
    row_count = queries.shape[0]
    key_heads = keys.shape[1] // HEAD_SIZE
    stacked_rows = queries.shape[1] // (key_heads * HEAD_SIZE) * row_count
    params = pltpu.CompilerParams(vmem_limit_bytes=vmem_bytes)
    old_keys = earlier_sections(keys, reach)
    old_values = earlier_sections(values, reach)
    like = lambda array: jax.ShapeDtypeStruct(array.shape, array.dtype)
    own_queries, own_values, weight, scores, bias = pl.pallas_call(
        own_kernel,
        out_shape=(
            like(queries),
            like(values),
            like(turned_weight),
            jax.ShapeDtypeStruct((key_heads, stacked_rows, row_count), jnp.float32),
            jax.ShapeDtypeStruct((row_count, reach * row_count), jnp.float32),
        ),
        in_specs=[in_hbm] * 5,
        out_specs=(in_vmem,) * 5,
        scratch_shapes=[
            pltpu.VMEM(keys.shape, keys.dtype),
            pltpu.SMEM(prefix.shape, prefix.dtype),
            pltpu.SemaphoreType.DMA((5,)),
        ],
        compiler_params=params,
        cost_estimate=no_cost,
        name="own_scores",
    )(*(pltpu.with_memory_space_constraint(array, pltpu.HBM) for array in (prefix, queries, keys, values, turned_weight)))
    half = jax.ShapeDtypeStruct((row_count // 2, queries.shape[1]), queries.dtype)
    attention = pl.pallas_call(
        rest_kernel,
        out_shape=(half, half) if in_halves else like(queries),
        in_specs=[in_vmem] * 6,
        out_specs=(in_vmem, in_vmem) if in_halves else in_vmem,
        scratch_shapes=[pltpu.VMEM(queries.shape, queries.dtype)] if in_halves else [],
        compiler_params=params,
        cost_estimate=no_cost,
        name="attend",
    )(own_queries, own_values, scores, bias, old_keys, old_values)
    return attention, weight


def project_kernel(chunk_count, *refs):
    chunk_refs = refs[:chunk_count]
    weight_refs = refs[chunk_count : chunk_count + 2]
    sent_ref, kept_ref = refs[-2:]
    product = sum(
        lax.dot_general(
            jnp.concatenate([chunk_ref[at] for chunk_ref in chunk_refs], axis=0),
            weight_ref[...],
            (((1,), (1,)), ((), ())),
            preferred_element_type=jnp.float32,
        )
        for at, weight_ref in enumerate(weight_refs)
    )
    rows = sent_ref.shape[1]
    for at in range(chunk_count):
        first = 2 * rows * at
        sent_ref[at] = product[first : first + rows].astype(jnp.bfloat16)
        kept_ref[at] = product[first + rows : first + 2 * rows]


def project(chunks, weights, earlier):
    shape = (len(chunks), chunks[0].shape[1] // 2, weights[0].shape[0])
    return pl.pallas_call(
        functools.partial(project_kernel, len(chunks)),
        out_shape=(
            jax.ShapeDtypeStruct(shape, jnp.bfloat16),
            jax.ShapeDtypeStruct(shape, jnp.float32),
        ),
        in_specs=[in_vmem] * (len(chunks) + 2) + [anywhere] * len(earlier),
        out_specs=(in_vmem, in_vmem),
        compiler_params=pltpu.CompilerParams(vmem_limit_bytes=vmem_bytes),
        cost_estimate=project_cost,
        name="project",
    )(*chunks, *weights, *earlier)


def relay_kernel(array_ref, _, out_ref):
    out_ref[...] = array_ref[...]


def after(array, earlier):
    return pl.pallas_call(
        relay_kernel,
        out_shape=jax.ShapeDtypeStruct(array.shape, array.dtype),
        in_specs=[in_vmem, anywhere],
        out_specs=in_vmem,
        compiler_params=pltpu.CompilerParams(vmem_limit_bytes=vmem_bytes),
        cost_estimate=no_cost,
        name="relay",
    )(array, earlier)


def squares_kernel(has_earlier, *refs):
    *piece_refs, out_ref = refs
    total = piece_refs.pop()[:, :1] if has_earlier else 0.0
    for piece_ref in piece_refs:
        piece = piece_ref[...].astype(jnp.float32)
        total = total + jnp.sum(piece * piece, axis=-1, keepdims=True)
    out_ref[...] = jnp.broadcast_to(total, out_ref.shape)


def squares(pieces, earlier):
    given = list(pieces) if earlier is None else [*pieces, earlier]
    return pl.pallas_call(
        functools.partial(squares_kernel, earlier is not None),
        out_shape=jax.ShapeDtypeStruct((pieces[0].shape[0], HEAD_SIZE), jnp.float32),
        in_specs=[in_vmem] * len(given),
        out_specs=in_vmem,
        compiler_params=pltpu.CompilerParams(vmem_limit_bytes=vmem_bytes),
        cost_estimate=no_cost,
        name="squares",
    )(*given)


def norm_kernel(count, *refs):
    piece_refs = refs[:count]
    squares_ref, residual_ref, gain_ref, out_ref, piece_ref = refs[count:]
    width = piece_ref.shape[2]
    for at, moved_ref in enumerate(piece_refs):
        piece_ref[at] = moved_ref[...].astype(jnp.float32)
    last = piece_ref[last_flip(count)]
    square = squares_ref[:, :1] + jnp.sum(last * last, axis=-1, keepdims=True)
    scale = lax.rsqrt(square / (count * width) + norm_eps)
    section_index = lax.axis_index("section")
    for at in range(count):
        place = slice(at * width, (at + 1) * width)
        normed = piece_ref[section_index ^ at] * scale * gain_ref[:, place]
        out_ref[:, place] = (residual_ref[:, place].astype(jnp.float32) + normed).astype(jnp.bfloat16)


def last_flip(section_total):
    return section_flips(section_total)[-1][-1]


def section_flips(section_total):
    return [[0], list(range(1, section_total - 1)), [section_total - 1]]


def norm(pieces, residual, post_gain):
    early = None
    for group in section_flips(len(pieces))[:-1]:
        early = squares([pieces[flip] for flip in group], early)
    return pl.pallas_call(
        functools.partial(norm_kernel, len(pieces)),
        out_shape=jax.ShapeDtypeStruct(residual.shape, jnp.bfloat16),
        in_specs=[in_vmem] * (len(pieces) + 3),
        out_specs=in_vmem,
        scratch_shapes=[pltpu.VMEM((len(pieces), *pieces[0].shape), jnp.float32)],
        compiler_params=pltpu.CompilerParams(vmem_limit_bytes=vmem_bytes),
        cost_estimate=no_cost,
        name="norm",
    )(*pieces, early, residual, post_gain[None, :])


def local(queries, token_key_rows, token_value_rows, residual, prefix, out_weight, post_gain):
    own_rows = residual.shape[0]
    section_total = lax.axis_size("section")
    head_total = lax.axis_size("head")
    reach = 3 * section_total // 8
    in_halves = (
        2 < section_total <= most_paired and is_power(section_total) and head_total == 4
    )
    turned = out_weight.T
    attention, turned_weight = attend(
        queries, token_key_rows, token_value_rows, prefix, turned, reach, in_halves
    )
    if in_halves:
        weights = [turned_weight, exchanged(turned, "head", 1)]
        sent, kept = attention
        gathered = {0: jnp.stack([kept, exchanged(sent, "head", 1)])}
        for flip in range(1, section_total):
            if is_power(flip):
                gathered[flip] = exchanged(gathered[0], "section", flip)
        sent, halves, arrivals = None, [], []
        groups = section_flips(section_total)
        for group in groups:
            for flip in group:
                if flip not in gathered:
                    lowest = flip & -flip
                    gathered[flip] = exchanged(gathered[flip ^ lowest], "section", lowest)
            chunks = [gathered[flip] for flip in group]
            sent, half = project(chunks, weights, [] if sent is None else [sent])
            halves.append(half)
            arrivals.append(exchanged(sent, "head", 2))
            if group is groups[0]:
                for flip in range(2, section_total):
                    if is_power(flip):
                        gathered[flip] = after(gathered[flip], sent)
        pieces = [None] * section_total
        for group, half, arrived in zip(groups, halves, arrivals, strict=True):
            for at, flip in enumerate(group):
                total = half[at] + arrived[at].astype(jnp.float32)
                if flip:
                    total = exchanged(total.astype(jnp.bfloat16), "section", flip)
                pieces[flip] = total
        return norm(pieces, residual, post_gain)
    gathered = lax.all_gather(attention, "section", axis=0, tiled=True)
    product = jnp.dot(gathered, turned_weight.T, preferred_element_type=jnp.float32)
    product = product.astype(jnp.bfloat16).reshape(-1, head_total, own_rows, product.shape[-1])
    sums = lax.psum_scatter(product, "head", scatter_dimension=1, tiled=False)
    pieces = lax.all_to_all(sums, "section", 0, 0)
    summed = jnp.transpose(pieces, (1, 0, 2)).reshape(own_rows, -1).astype(jnp.float32)
    mean_square = jnp.mean(summed * summed, axis=-1, keepdims=True)
    normed = summed * lax.rsqrt(mean_square + norm_eps) * post_gain[None, :]
    return (residual.astype(jnp.float32) + normed).astype(jnp.bfloat16)


def solution(mesh):
    placed = (
        P(("groups", "section"), "head"),
        P(("groups", "section"), "head"),
        P(("groups", "section"), "head"),
        P(("groups", "section", "head"), None),
        P("groups"),
        P("head", "section"),
        P(),
    )
    return jax.shard_map(
        local,
        mesh=mesh,
        in_specs=placed,
        out_specs=P(("groups", "section", "head"), None),
        check_vma=False,
    )
```

```python
import functools

import jax
import jax.numpy as jnp
from jax import lax
from jax.experimental import pallas as pl
from jax.experimental.pallas import tpu as pltpu
from jax.sharding import PartitionSpec as P

HEAD_SIZE = 128


score_scale = 168.0 ** (-0.5)
floor_value = -1e30
norm_eps = 1e-06
vmem_bytes = 24 * 2**20
owner_flips = ((3, 1), (2, 0))
most_paired = 8

in_vmem = pl.BlockSpec(memory_space=pltpu.VMEM)
in_smem = pl.BlockSpec(memory_space=pltpu.SMEM)
in_hbm = pl.BlockSpec(memory_space=pltpu.HBM)
anywhere = pl.BlockSpec(memory_space=pl.ANY)


no_cost = pl.CostEstimate(flops=0, transcendentals=0, bytes_accessed=0)
project_cost = pl.CostEstimate(flops=3 * 10**9, transcendentals=0, bytes_accessed=0)


def is_power(count):
    return count & (count - 1) == 0


def rotated(value, axis, steps):
    count = lax.axis_size(axis)
    return lax.ppermute(value, axis, [(at, (at + steps) % count) for at in range(count)])


def exchanged(value, axis, flip):
    count = lax.axis_size(axis)
    return lax.ppermute(value, axis, [(at, at ^ flip) for at in range(count)])


def earlier_sections(own_rows, reach):
    held = own_rows[None]
    stride = 1
    while stride <= reach:
        moved_count = min(stride, reach + 1 - stride)
        held = jnp.concatenate([held, rotated(held[:moved_count], "section", stride)], axis=0)
        stride = stride * 2
    return held[:0:-1].reshape(reach * own_rows.shape[0], own_rows.shape[1])


def head_columns(head):
    return slice(head * HEAD_SIZE, (head + 1) * HEAD_SIZE)


def stacked_queries(query_ref, key_head, group_width):
    first = key_head * group_width
    return jnp.concatenate(
        [query_ref[:, head_columns(head)] for head in range(first, first + group_width)], axis=0
    )


def scaled_scores(queries, keys):
    product = lax.dot_general(
        queries, keys, (((1,), (1,)), ((), ())), preferred_element_type=jnp.float32
    )
    return product * score_scale


def own_kernel(
    prefix_in,
    query_in,
    key_in,
    value_in,
    weight_in,
    query_ref,
    value_ref,
    weight_ref,
    score_ref,
    bias_ref,
    key_ref,
    prefix_ref,
    sems,
):
    loads = [
        pltpu.make_async_copy(source, target, sems.at[at])
        for at, (source, target) in enumerate(
            (
                (prefix_in, prefix_ref),
                (query_in, query_ref),
                (key_in, key_ref),
                (value_in, value_ref),
                (weight_in, weight_ref),
            )
        )
    ]
    for load in loads:
        load.start()
    row_count = query_ref.shape[0]
    key_heads = key_ref.shape[1] // HEAD_SIZE
    group_width = query_ref.shape[1] // (key_heads * HEAD_SIZE)
    shape = (row_count, row_count)
    visible = lax.broadcasted_iota(jnp.int32, shape, 1) <= lax.broadcasted_iota(jnp.int32, shape, 0)
    visible = jnp.concatenate([visible] * group_width, axis=0)
    for load in loads[:3]:
        load.wait()
    section_index = lax.axis_index("section")
    seen_tokens = jnp.minimum(section_index * row_count, prefix_ref[section_index])
    old_pos = lax.broadcasted_iota(jnp.int32, bias_ref.shape, 1) - bias_ref.shape[1]
    bias_ref[...] = jnp.where(old_pos >= -seen_tokens, 0.0, floor_value)
    for key_head in range(key_heads):
        queries = stacked_queries(query_ref, key_head, group_width)
        scores = scaled_scores(queries, key_ref[:, head_columns(key_head)])
        score_ref[key_head] = jnp.where(visible, scores, floor_value)
    for load in loads[3:]:
        load.wait()


def weigh_kernel(query_ref, score_ref, bias_ref, old_key_ref, prob_ref, scale_ref):
    row_count = query_ref.shape[0]
    group_width = score_ref.shape[1] // row_count
    bias = jnp.concatenate([bias_ref[...]] * group_width, axis=0)
    for key_head in range(score_ref.shape[0]):
        queries = stacked_queries(query_ref, key_head, group_width)
        old_scores = scaled_scores(queries, old_key_ref[:, head_columns(key_head)]) + bias
        masked = jnp.concatenate([old_scores, score_ref[key_head]], axis=1)
        row_max = jnp.max(masked, axis=-1, keepdims=True)
        probs = jnp.exp(masked - row_max)
        denominator = jnp.sum(probs, axis=-1, keepdims=True)
        prob_ref[key_head] = probs.astype(jnp.bfloat16)
        scale_ref[key_head] = jnp.broadcast_to(1.0 / denominator, scale_ref.shape[1:])


def combine_kernel(prob_ref, scale_ref, value_ref, old_value_ref, *out_refs):
    whole_ref = out_refs[-1]
    row_count = whole_ref.shape[0]
    group_width = prob_ref.shape[1] // row_count
    for key_head in range(prob_ref.shape[0]):
        columns = head_columns(key_head)
        values = jnp.concatenate([old_value_ref[:, columns], value_ref[:, columns]], axis=0)
        combined = jnp.dot(prob_ref[key_head], values, preferred_element_type=jnp.float32)
        combined = (combined * scale_ref[key_head]).astype(jnp.bfloat16)
        for member in range(group_width):
            rows = slice(member * row_count, (member + 1) * row_count)
            whole_ref[:, head_columns(key_head * group_width + member)] = combined[rows]
    if len(out_refs) > 1:
        head_index = lax.axis_index("head")
        for out_ref, flips in zip(out_refs[:2], owner_flips, strict=True):
            own_rows = out_ref.shape[0] // len(flips)
            for at, flip in enumerate(flips):
                first = pl.multiple_of((head_index ^ flip) * own_rows, own_rows)
                out_ref[at * own_rows : (at + 1) * own_rows] = whole_ref[pl.ds(first, own_rows), :]


def attend(queries, keys, values, prefix, turned_weight, reach, in_halves):
    row_count = queries.shape[0]
    key_heads = keys.shape[1] // HEAD_SIZE
    stacked_rows = queries.shape[1] // (key_heads * HEAD_SIZE) * row_count
    params = pltpu.CompilerParams(vmem_limit_bytes=vmem_bytes)
    old_keys = earlier_sections(keys, reach)
    old_values = earlier_sections(values, reach)
    like = lambda array: jax.ShapeDtypeStruct(array.shape, array.dtype)
    own_queries, own_values, weight, scores, bias = pl.pallas_call(
        own_kernel,
        out_shape=(
            like(queries),
            like(values),
            like(turned_weight),
            jax.ShapeDtypeStruct((key_heads, stacked_rows, row_count), jnp.float32),
            jax.ShapeDtypeStruct((row_count, reach * row_count), jnp.float32),
        ),
        in_specs=[in_hbm] * 5,
        out_specs=(in_vmem,) * 5,
        scratch_shapes=[
            pltpu.VMEM(keys.shape, keys.dtype),
            pltpu.SMEM(prefix.shape, prefix.dtype),
            pltpu.SemaphoreType.DMA((5,)),
        ],
        compiler_params=params,
        cost_estimate=no_cost,
        name="own_scores",
    )(*(pltpu.with_memory_space_constraint(array, pltpu.HBM) for array in (prefix, queries, keys, values, turned_weight)))
    half = jax.ShapeDtypeStruct((row_count // 2, queries.shape[1]), queries.dtype)
    probs, scales = pl.pallas_call(
        weigh_kernel,
        out_shape=(
            jax.ShapeDtypeStruct(
                (key_heads, stacked_rows, (reach + 1) * row_count), jnp.bfloat16
            ),
            jax.ShapeDtypeStruct((key_heads, stacked_rows, HEAD_SIZE), jnp.float32),
        ),
        in_specs=[in_vmem] * 4,
        out_specs=(in_vmem,) * 2,
        compiler_params=params,
        cost_estimate=no_cost,
        name="weigh",
    )(own_queries, scores, bias, old_keys)
    attention = pl.pallas_call(
        combine_kernel,
        out_shape=(half, half) if in_halves else like(queries),
        in_specs=[in_vmem] * 4,
        out_specs=(in_vmem, in_vmem) if in_halves else in_vmem,
        scratch_shapes=[pltpu.VMEM(queries.shape, queries.dtype)] if in_halves else [],
        compiler_params=params,
        cost_estimate=no_cost,
        name="attend",
    )(probs, scales, own_values, old_values)
    return attention, weight


def project_kernel(chunk_count, *refs):
    chunk_refs = refs[:chunk_count]
    weight_refs = refs[chunk_count : chunk_count + 2]
    sent_ref, kept_ref = refs[-2:]
    product = sum(
        lax.dot_general(
            jnp.concatenate([chunk_ref[at] for chunk_ref in chunk_refs], axis=0),
            weight_ref[...],
            (((1,), (1,)), ((), ())),
            preferred_element_type=jnp.float32,
        )
        for at, weight_ref in enumerate(weight_refs)
    )
    rows = sent_ref.shape[1]
    for at in range(chunk_count):
        first = 2 * rows * at
        sent_ref[at] = product[first : first + rows].astype(jnp.bfloat16)
        kept_ref[at] = product[first + rows : first + 2 * rows]


def project(chunks, weights, earlier):
    shape = (len(chunks), chunks[0].shape[1] // 2, weights[0].shape[0])
    return pl.pallas_call(
        functools.partial(project_kernel, len(chunks)),
        out_shape=(
            jax.ShapeDtypeStruct(shape, jnp.bfloat16),
            jax.ShapeDtypeStruct(shape, jnp.float32),
        ),
        in_specs=[in_vmem] * (len(chunks) + 2) + [anywhere] * len(earlier),
        out_specs=(in_vmem, in_vmem),
        compiler_params=pltpu.CompilerParams(vmem_limit_bytes=vmem_bytes),
        cost_estimate=project_cost,
        name="project",
    )(*chunks, *weights, *earlier)


def relay_kernel(array_ref, _, out_ref):
    out_ref[...] = array_ref[...]


def after(array, earlier):
    return pl.pallas_call(
        relay_kernel,
        out_shape=jax.ShapeDtypeStruct(array.shape, array.dtype),
        in_specs=[in_vmem, anywhere],
        out_specs=in_vmem,
        compiler_params=pltpu.CompilerParams(vmem_limit_bytes=vmem_bytes),
        cost_estimate=no_cost,
        name="relay",
    )(array, earlier)


def squares_kernel(has_earlier, *refs):
    *piece_refs, out_ref = refs
    total = piece_refs.pop()[:, :1] if has_earlier else 0.0
    for piece_ref in piece_refs:
        piece = piece_ref[...].astype(jnp.float32)
        total = total + jnp.sum(piece * piece, axis=-1, keepdims=True)
    out_ref[...] = jnp.broadcast_to(total, out_ref.shape)


def squares(pieces, earlier):
    given = list(pieces) if earlier is None else [*pieces, earlier]
    return pl.pallas_call(
        functools.partial(squares_kernel, earlier is not None),
        out_shape=jax.ShapeDtypeStruct((pieces[0].shape[0], HEAD_SIZE), jnp.float32),
        in_specs=[in_vmem] * len(given),
        out_specs=in_vmem,
        compiler_params=pltpu.CompilerParams(vmem_limit_bytes=vmem_bytes),
        cost_estimate=no_cost,
        name="squares",
    )(*given)


def norm_kernel(count, *refs):
    piece_refs = refs[:count]
    squares_ref, residual_ref, gain_ref, out_ref, piece_ref = refs[count:]
    width = piece_ref.shape[2]
    for at, moved_ref in enumerate(piece_refs):
        piece_ref[at] = moved_ref[...].astype(jnp.float32)
    last = piece_ref[last_flip(count)]
    square = squares_ref[:, :1] + jnp.sum(last * last, axis=-1, keepdims=True)
    scale = lax.rsqrt(square / (count * width) + norm_eps)
    section_index = lax.axis_index("section")
    for at in range(count):
        place = slice(at * width, (at + 1) * width)
        normed = piece_ref[section_index ^ at] * scale * gain_ref[:, place]
        out_ref[:, place] = (residual_ref[:, place].astype(jnp.float32) + normed).astype(jnp.bfloat16)


def last_flip(section_total):
    return section_flips(section_total)[-1][-1]


def section_flips(section_total):
    return [[0], list(range(1, section_total - 1)), [section_total - 1]]


def norm(pieces, residual, post_gain):
    early = None
    for group in section_flips(len(pieces))[:-1]:
        early = squares([pieces[flip] for flip in group], early)
    return pl.pallas_call(
        functools.partial(norm_kernel, len(pieces)),
        out_shape=jax.ShapeDtypeStruct(residual.shape, jnp.bfloat16),
        in_specs=[in_vmem] * (len(pieces) + 3),
        out_specs=in_vmem,
        scratch_shapes=[pltpu.VMEM((len(pieces), *pieces[0].shape), jnp.float32)],
        compiler_params=pltpu.CompilerParams(vmem_limit_bytes=vmem_bytes),
        cost_estimate=no_cost,
        name="norm",
    )(*pieces, early, residual, post_gain[None, :])


def local(queries, token_key_rows, token_value_rows, residual, prefix, out_weight, post_gain):
    own_rows = residual.shape[0]
    section_total = lax.axis_size("section")
    head_total = lax.axis_size("head")
    reach = 3 * section_total // 8
    in_halves = (
        2 < section_total <= most_paired and is_power(section_total) and head_total == 4
    )
    turned = out_weight.T
    attention, turned_weight = attend(
        queries, token_key_rows, token_value_rows, prefix, turned, reach, in_halves
    )
    if in_halves:
        weights = [turned_weight, exchanged(turned, "head", 1)]
        sent, kept = attention
        gathered = {0: jnp.stack([kept, exchanged(sent, "head", 1)])}
        for flip in range(1, section_total):
            if is_power(flip):
                gathered[flip] = exchanged(gathered[0], "section", flip)
        sent, halves, arrivals = None, [], []
        groups = section_flips(section_total)
        for group in groups:
            for flip in group:
                if flip not in gathered:
                    lowest = flip & -flip
                    gathered[flip] = exchanged(gathered[flip ^ lowest], "section", lowest)
            chunks = [gathered[flip] for flip in group]
            sent, half = project(chunks, weights, [] if sent is None else [sent])
            halves.append(half)
            arrivals.append(exchanged(sent, "head", 2))
            if group is groups[0]:
                for flip in range(2, section_total):
                    if is_power(flip):
                        gathered[flip] = after(gathered[flip], sent)
        pieces = [None] * section_total
        for group, half, arrived in zip(groups, halves, arrivals, strict=True):
            for at, flip in enumerate(group):
                total = half[at] + arrived[at].astype(jnp.float32)
                if flip:
                    total = exchanged(total.astype(jnp.bfloat16), "section", flip)
                pieces[flip] = total
        return norm(pieces, residual, post_gain)
    gathered = lax.all_gather(attention, "section", axis=0, tiled=True)
    product = jnp.dot(gathered, turned_weight.T, preferred_element_type=jnp.float32)
    product = product.astype(jnp.bfloat16).reshape(-1, head_total, own_rows, product.shape[-1])
    sums = lax.psum_scatter(product, "head", scatter_dimension=1, tiled=False)
    pieces = lax.all_to_all(sums, "section", 0, 0)
    summed = jnp.transpose(pieces, (1, 0, 2)).reshape(own_rows, -1).astype(jnp.float32)
    mean_square = jnp.mean(summed * summed, axis=-1, keepdims=True)
    normed = summed * lax.rsqrt(mean_square + norm_eps) * post_gain[None, :]
    return (residual.astype(jnp.float32) + normed).astype(jnp.bfloat16)


def solution(mesh):
    placed = (
        P(("groups", "section"), "head"),
        P(("groups", "section"), "head"),
        P(("groups", "section"), "head"),
        P(("groups", "section", "head"), None),
        P("groups"),
        P("head", "section"),
        P(),
    )
    return jax.shard_map(
        local,
        mesh=mesh,
        in_specs=placed,
        out_specs=P(("groups", "section", "head"), None),
        check_vma=False,
    )
```

```python
import functools

import jax
import jax.numpy as jnp
from jax import lax
from jax.experimental import pallas as pl
from jax.experimental.pallas import tpu as pltpu
from jax.sharding import PartitionSpec as P

HEAD_SIZE = 128


score_scale = 168.0 ** (-0.5)
floor_value = -1e30
norm_eps = 1e-06
vmem_bytes = 24 * 2**20
owner_flips = ((3, 1), (2, 0))
most_paired = 8

in_vmem = pl.BlockSpec(memory_space=pltpu.VMEM)
in_smem = pl.BlockSpec(memory_space=pltpu.SMEM)
in_hbm = pl.BlockSpec(memory_space=pltpu.HBM)
anywhere = pl.BlockSpec(memory_space=pl.ANY)


no_cost = pl.CostEstimate(flops=0, transcendentals=0, bytes_accessed=0)
project_cost = pl.CostEstimate(flops=3 * 10**9, transcendentals=0, bytes_accessed=0)


def is_power(count):
    return count & (count - 1) == 0


def rotated(value, axis, steps):
    count = lax.axis_size(axis)
    return lax.ppermute(value, axis, [(at, (at + steps) % count) for at in range(count)])


def exchanged(value, axis, flip):
    count = lax.axis_size(axis)
    return lax.ppermute(value, axis, [(at, at ^ flip) for at in range(count)])


def crossed(value, flip):
    sections, heads = lax.axis_size("section"), lax.axis_size("head")
    pairs = [
        (section * heads + head, (section ^ flip) * heads + (head ^ 1))
        for section in range(sections)
        for head in range(heads)
    ]
    return lax.ppermute(value, ("section", "head"), pairs)


def earlier_sections(own_rows, reach):
    held = own_rows[None]
    stride = 1
    while stride <= reach:
        moved_count = min(stride, reach + 1 - stride)
        held = jnp.concatenate([held, rotated(held[:moved_count], "section", stride)], axis=0)
        stride = stride * 2
    return held[:0:-1].reshape(reach * own_rows.shape[0], own_rows.shape[1])


def head_columns(head):
    return slice(head * HEAD_SIZE, (head + 1) * HEAD_SIZE)


def stacked_queries(query_ref, key_head, group_width):
    first = key_head * group_width
    return jnp.concatenate(
        [query_ref[:, head_columns(head)] for head in range(first, first + group_width)], axis=0
    )


def scaled_scores(queries, keys):
    product = lax.dot_general(
        queries, keys, (((1,), (1,)), ((), ())), preferred_element_type=jnp.float32
    )
    return product * score_scale


def own_kernel(
    prefix_in,
    query_in,
    key_in,
    value_in,
    weight_in,
    query_ref,
    value_ref,
    weight_ref,
    score_ref,
    bias_ref,
    key_ref,
    prefix_ref,
    sems,
):
    loads = [
        pltpu.make_async_copy(source, target, sems.at[at])
        for at, (source, target) in enumerate(
            (
                (prefix_in, prefix_ref),
                (query_in, query_ref),
                (key_in, key_ref),
                (value_in, value_ref),
                (weight_in, weight_ref),
            )
        )
    ]
    for load in loads:
        load.start()
    row_count = query_ref.shape[0]
    key_heads = key_ref.shape[1] // HEAD_SIZE
    group_width = query_ref.shape[1] // (key_heads * HEAD_SIZE)
    shape = (row_count, row_count)
    visible = lax.broadcasted_iota(jnp.int32, shape, 1) <= lax.broadcasted_iota(jnp.int32, shape, 0)
    visible = jnp.concatenate([visible] * group_width, axis=0)
    for load in loads[:3]:
        load.wait()
    section_index = lax.axis_index("section")
    seen_tokens = jnp.minimum(section_index * row_count, prefix_ref[section_index])
    old_pos = lax.broadcasted_iota(jnp.int32, bias_ref.shape, 1) - bias_ref.shape[1]
    bias_ref[...] = jnp.where(old_pos >= -seen_tokens, 0.0, floor_value)
    for key_head in range(key_heads):
        queries = stacked_queries(query_ref, key_head, group_width)
        scores = scaled_scores(queries, key_ref[:, head_columns(key_head)])
        score_ref[key_head] = jnp.where(visible, scores, floor_value)
    for load in loads[3:]:
        load.wait()


def weigh_kernel(query_ref, score_ref, bias_ref, old_key_ref, prob_ref, scale_ref):
    row_count = query_ref.shape[0]
    group_width = score_ref.shape[1] // row_count
    bias = jnp.concatenate([bias_ref[...]] * group_width, axis=0)
    for key_head in range(score_ref.shape[0]):
        queries = stacked_queries(query_ref, key_head, group_width)
        old_scores = scaled_scores(queries, old_key_ref[:, head_columns(key_head)]) + bias
        masked = jnp.concatenate([old_scores, score_ref[key_head]], axis=1)
        row_max = jnp.max(masked, axis=-1, keepdims=True)
        probs = jnp.exp(masked - row_max)
        denominator = jnp.sum(probs, axis=-1, keepdims=True)
        prob_ref[key_head] = probs.astype(jnp.bfloat16)
        scale_ref[key_head] = jnp.broadcast_to(1.0 / denominator, scale_ref.shape[1:])


def combine_kernel(prob_ref, scale_ref, value_ref, old_value_ref, *out_refs):
    whole_ref = out_refs[-1]
    row_count = whole_ref.shape[0]
    group_width = prob_ref.shape[1] // row_count
    for key_head in range(prob_ref.shape[0]):
        columns = head_columns(key_head)
        values = jnp.concatenate([old_value_ref[:, columns], value_ref[:, columns]], axis=0)
        combined = jnp.dot(prob_ref[key_head], values, preferred_element_type=jnp.float32)
        combined = (combined * scale_ref[key_head]).astype(jnp.bfloat16)
        for member in range(group_width):
            rows = slice(member * row_count, (member + 1) * row_count)
            whole_ref[:, head_columns(key_head * group_width + member)] = combined[rows]
    if len(out_refs) > 1:
        head_index = lax.axis_index("head")
        for out_ref, flips in zip(out_refs[:2], owner_flips, strict=True):
            own_rows = out_ref.shape[0] // len(flips)
            for at, flip in enumerate(flips):
                first = pl.multiple_of((head_index ^ flip) * own_rows, own_rows)
                out_ref[at * own_rows : (at + 1) * own_rows] = whole_ref[pl.ds(first, own_rows), :]


def attend(queries, keys, values, prefix, turned_weight, reach, in_halves):
    row_count = queries.shape[0]
    key_heads = keys.shape[1] // HEAD_SIZE
    stacked_rows = queries.shape[1] // (key_heads * HEAD_SIZE) * row_count
    params = pltpu.CompilerParams(vmem_limit_bytes=vmem_bytes)
    old_keys = earlier_sections(keys, reach)
    old_values = earlier_sections(values, reach)
    like = lambda array: jax.ShapeDtypeStruct(array.shape, array.dtype)
    own_queries, own_values, weight, scores, bias = pl.pallas_call(
        own_kernel,
        out_shape=(
            like(queries),
            like(values),
            like(turned_weight),
            jax.ShapeDtypeStruct((key_heads, stacked_rows, row_count), jnp.float32),
            jax.ShapeDtypeStruct((row_count, reach * row_count), jnp.float32),
        ),
        in_specs=[in_hbm] * 5,
        out_specs=(in_vmem,) * 5,
        scratch_shapes=[
            pltpu.VMEM(keys.shape, keys.dtype),
            pltpu.SMEM(prefix.shape, prefix.dtype),
            pltpu.SemaphoreType.DMA((5,)),
        ],
        compiler_params=params,
        cost_estimate=no_cost,
        name="own_scores",
    )(*(pltpu.with_memory_space_constraint(array, pltpu.HBM) for array in (prefix, queries, keys, values, turned_weight)))
    half = jax.ShapeDtypeStruct((row_count // 2, queries.shape[1]), queries.dtype)
    probs, scales = pl.pallas_call(
        weigh_kernel,
        out_shape=(
            jax.ShapeDtypeStruct(
                (key_heads, stacked_rows, (reach + 1) * row_count), jnp.bfloat16
            ),
            jax.ShapeDtypeStruct((key_heads, stacked_rows, HEAD_SIZE), jnp.float32),
        ),
        in_specs=[in_vmem] * 4,
        out_specs=(in_vmem,) * 2,
        compiler_params=params,
        cost_estimate=no_cost,
        name="weigh",
    )(own_queries, scores, bias, old_keys)
    attention = pl.pallas_call(
        combine_kernel,
        out_shape=(half, half) if in_halves else like(queries),
        in_specs=[in_vmem] * 4,
        out_specs=(in_vmem, in_vmem) if in_halves else in_vmem,
        scratch_shapes=[pltpu.VMEM(queries.shape, queries.dtype)] if in_halves else [],
        compiler_params=params,
        cost_estimate=no_cost,
        name="attend",
    )(probs, scales, own_values, old_values)
    return attention, weight


def project_kernel(counts, *refs):
    chunks = []
    for count in counts:
        chunk, refs = refs[:count], refs[count:]
        chunks.append(chunk if count == 2 else [chunk[0].at[0], chunk[0].at[1]])
    weight_refs, sent_ref, kept_ref = refs[:2], *refs[-2:]
    product = sum(
        lax.dot_general(
            jnp.concatenate([chunk[at][...] for chunk in chunks], axis=0),
            weight_ref[...],
            (((1,), (1,)), ((), ())),
            preferred_element_type=jnp.float32,
        )
        for at, weight_ref in enumerate(weight_refs)
    )
    rows = sent_ref.shape[1]
    for at in range(len(chunks)):
        first = 2 * rows * at
        sent_ref[at] = product[first : first + rows].astype(jnp.bfloat16)
        kept_ref[at] = product[first + rows : first + 2 * rows]


def project(chunks, weights, earlier):
    shape = (len(chunks), chunks[0][0].shape[-2] // 2, weights[0].shape[0])
    given = [array for chunk in chunks for array in chunk] + list(weights)
    return pl.pallas_call(
        functools.partial(project_kernel, [len(chunk) for chunk in chunks]),
        out_shape=(
            jax.ShapeDtypeStruct(shape, jnp.bfloat16),
            jax.ShapeDtypeStruct(shape, jnp.float32),
        ),
        in_specs=[in_vmem] * len(given) + [anywhere] * len(earlier),
        out_specs=(in_vmem, in_vmem),
        compiler_params=pltpu.CompilerParams(vmem_limit_bytes=vmem_bytes),
        cost_estimate=project_cost,
        name="project",
    )(*given, *earlier)


def stack_kernel(own_ref, other_ref, _, out_ref):
    out_ref[0] = own_ref[...]
    out_ref[1] = other_ref[...]


def stacked_after(own, other, earlier):
    return pl.pallas_call(
        stack_kernel,
        out_shape=jax.ShapeDtypeStruct((2, *own.shape), own.dtype),
        in_specs=[in_vmem, in_vmem, anywhere],
        out_specs=in_vmem,
        compiler_params=pltpu.CompilerParams(vmem_limit_bytes=vmem_bytes),
        cost_estimate=no_cost,
        name="stack",
    )(own, other, earlier)


def squares_kernel(has_earlier, *refs):
    *piece_refs, out_ref = refs
    total = piece_refs.pop()[:, :1] if has_earlier else 0.0
    for piece_ref in piece_refs:
        piece = piece_ref[...].astype(jnp.float32)
        total = total + jnp.sum(piece * piece, axis=-1, keepdims=True)
    out_ref[...] = jnp.broadcast_to(total, out_ref.shape)


def squares(pieces, earlier):
    given = list(pieces) if earlier is None else [*pieces, earlier]
    return pl.pallas_call(
        functools.partial(squares_kernel, earlier is not None),
        out_shape=jax.ShapeDtypeStruct((pieces[0].shape[0], HEAD_SIZE), jnp.float32),
        in_specs=[in_vmem] * len(given),
        out_specs=in_vmem,
        compiler_params=pltpu.CompilerParams(vmem_limit_bytes=vmem_bytes),
        cost_estimate=no_cost,
        name="squares",
    )(*given)


def norm_kernel(count, *refs):
    piece_refs = refs[:count]
    squares_ref, residual_ref, gain_ref, out_ref, piece_ref = refs[count:]
    width = piece_ref.shape[2]
    for at, moved_ref in enumerate(piece_refs):
        piece_ref[at] = moved_ref[...].astype(jnp.float32)
    last = piece_ref[last_flip(count)]
    square = squares_ref[:, :1] + jnp.sum(last * last, axis=-1, keepdims=True)
    scale = lax.rsqrt(square / (count * width) + norm_eps)
    section_index = lax.axis_index("section")
    for at in range(count):
        place = slice(at * width, (at + 1) * width)
        normed = piece_ref[section_index ^ at] * scale * gain_ref[:, place]
        out_ref[:, place] = (residual_ref[:, place].astype(jnp.float32) + normed).astype(jnp.bfloat16)


def last_flip(section_total):
    return section_flips(section_total)[-1][-1]


def section_flips(section_total):
    return [[0], list(range(1, section_total - 1)), [section_total - 1]]


def norm(pieces, residual, post_gain):
    early = None
    for group in section_flips(len(pieces))[:-1]:
        early = squares([pieces[flip] for flip in group], early)
    return pl.pallas_call(
        functools.partial(norm_kernel, len(pieces)),
        out_shape=jax.ShapeDtypeStruct(residual.shape, jnp.bfloat16),
        in_specs=[in_vmem] * (len(pieces) + 3),
        out_specs=in_vmem,
        scratch_shapes=[pltpu.VMEM((len(pieces), *pieces[0].shape), jnp.float32)],
        compiler_params=pltpu.CompilerParams(vmem_limit_bytes=vmem_bytes),
        cost_estimate=no_cost,
        name="norm",
    )(*pieces, early, residual, post_gain[None, :])


def local(queries, token_key_rows, token_value_rows, residual, prefix, out_weight, post_gain):
    own_rows = residual.shape[0]
    section_total = lax.axis_size("section")
    head_total = lax.axis_size("head")
    reach = 3 * section_total // 8
    in_halves = (
        2 < section_total <= most_paired and is_power(section_total) and head_total == 4
    )
    turned = out_weight.T
    attention, turned_weight = attend(
        queries, token_key_rows, token_value_rows, prefix, turned, reach, in_halves
    )
    if in_halves:
        weights = [turned_weight, exchanged(turned, "head", 1)]
        sent, kept = attention
        whole = jnp.stack([kept, exchanged(sent, "head", 1)])
        gathered = {0: [whole], 1: [exchanged(whole, "section", 1)]}
        for flip in range(2, section_total):
            if is_power(flip):
                gathered[flip] = [exchanged(kept, "section", flip), crossed(sent, flip)]
        sent, halves, arrivals = None, [], []
        groups = section_flips(section_total)
        for group in groups:
            for flip in group:
                if flip not in gathered:
                    lowest = flip & -flip
                    [source] = gathered[flip ^ lowest]
                    gathered[flip] = [exchanged(source, "section", lowest)]
            chunks = [gathered[flip] for flip in group]
            sent, half = project(chunks, weights, [] if sent is None else [sent])
            halves.append(half)
            arrivals.append(exchanged(sent, "head", 2))
            if group is groups[0]:
                for flip in range(2, section_total):
                    if is_power(flip):
                        gathered[flip] = [stacked_after(*gathered[flip], sent)]
        pieces = [None] * section_total
        for group, half, arrived in zip(groups, halves, arrivals, strict=True):
            for at, flip in enumerate(group):
                total = half[at] + arrived[at].astype(jnp.float32)
                if flip:
                    total = exchanged(total.astype(jnp.bfloat16), "section", flip)
                pieces[flip] = total
        return norm(pieces, residual, post_gain)
    gathered = lax.all_gather(attention, "section", axis=0, tiled=True)
    product = jnp.dot(gathered, turned_weight.T, preferred_element_type=jnp.float32)
    product = product.astype(jnp.bfloat16).reshape(-1, head_total, own_rows, product.shape[-1])
    sums = lax.psum_scatter(product, "head", scatter_dimension=1, tiled=False)
    pieces = lax.all_to_all(sums, "section", 0, 0)
    summed = jnp.transpose(pieces, (1, 0, 2)).reshape(own_rows, -1).astype(jnp.float32)
    mean_square = jnp.mean(summed * summed, axis=-1, keepdims=True)
    normed = summed * lax.rsqrt(mean_square + norm_eps) * post_gain[None, :]
    return (residual.astype(jnp.float32) + normed).astype(jnp.bfloat16)


def solution(mesh):
    placed = (
        P(("groups", "section"), "head"),
        P(("groups", "section"), "head"),
        P(("groups", "section"), "head"),
        P(("groups", "section", "head"), None),
        P("groups"),
        P("head", "section"),
        P(),
    )
    return jax.shard_map(
        local,
        mesh=mesh,
        in_specs=placed,
        out_specs=P(("groups", "section", "head"), None),
        check_vma=False,
    )
```

```python
import functools

import jax
import jax.numpy as jnp
from jax import lax
from jax.experimental import pallas as pl
from jax.experimental.pallas import tpu as pltpu
from jax.sharding import PartitionSpec as P

HEAD_SIZE = 128


score_scale = 168.0 ** (-0.5)
floor_value = -1e30
norm_eps = 1e-06
vmem_bytes = 24 * 2**20
owner_flips = ((3, 1), (2, 0))
most_paired = 8

in_vmem = pl.BlockSpec(memory_space=pltpu.VMEM)
in_smem = pl.BlockSpec(memory_space=pltpu.SMEM)
in_hbm = pl.BlockSpec(memory_space=pltpu.HBM)
anywhere = pl.BlockSpec(memory_space=pl.ANY)


no_cost = pl.CostEstimate(flops=0, transcendentals=0, bytes_accessed=0)
project_cost = pl.CostEstimate(flops=3 * 10**9, transcendentals=0, bytes_accessed=0)


def is_power(count):
    return count & (count - 1) == 0


def rotated(value, axis, steps):
    count = lax.axis_size(axis)
    return lax.ppermute(value, axis, [(at, (at + steps) % count) for at in range(count)])


def exchanged(value, axis, flip):
    count = lax.axis_size(axis)
    return lax.ppermute(value, axis, [(at, at ^ flip) for at in range(count)])


def crossed(value, flip):
    sections, heads = lax.axis_size("section"), lax.axis_size("head")
    pairs = [
        (section * heads + head, (section ^ flip) * heads + (head ^ 1))
        for section in range(sections)
        for head in range(heads)
    ]
    return lax.ppermute(value, ("section", "head"), pairs)


def earlier_sections(own_rows, reach):
    held = own_rows[None]
    stride = 1
    while stride <= reach:
        moved_count = min(stride, reach + 1 - stride)
        held = jnp.concatenate([held, rotated(held[:moved_count], "section", stride)], axis=0)
        stride = stride * 2
    return held[:0:-1].reshape(reach * own_rows.shape[0], own_rows.shape[1])


def head_columns(head):
    return slice(head * HEAD_SIZE, (head + 1) * HEAD_SIZE)


def stacked_queries(query_ref, key_head, group_width):
    first = key_head * group_width
    return jnp.concatenate(
        [query_ref[:, head_columns(head)] for head in range(first, first + group_width)], axis=0
    )


def scaled_scores(queries, keys):
    product = lax.dot_general(
        queries, keys, (((1,), (1,)), ((), ())), preferred_element_type=jnp.float32
    )
    return product * score_scale


def own_kernel(
    prefix_in,
    query_in,
    key_in,
    value_in,
    weight_in,
    query_ref,
    value_ref,
    weight_ref,
    score_ref,
    bias_ref,
    key_ref,
    prefix_ref,
    sems,
):
    loads = [
        pltpu.make_async_copy(source, target, sems.at[at])
        for at, (source, target) in enumerate(
            (
                (prefix_in, prefix_ref),
                (query_in, query_ref),
                (key_in, key_ref),
                (value_in, value_ref),
                (weight_in, weight_ref),
            )
        )
    ]
    for load in loads:
        load.start()
    row_count = query_ref.shape[0]
    key_heads = key_ref.shape[1] // HEAD_SIZE
    group_width = query_ref.shape[1] // (key_heads * HEAD_SIZE)
    shape = (row_count, row_count)
    visible = lax.broadcasted_iota(jnp.int32, shape, 1) <= lax.broadcasted_iota(jnp.int32, shape, 0)
    visible = jnp.concatenate([visible] * group_width, axis=0)
    for load in loads[:3]:
        load.wait()
    section_index = lax.axis_index("section")
    seen_tokens = jnp.minimum(section_index * row_count, prefix_ref[section_index])
    old_pos = lax.broadcasted_iota(jnp.int32, bias_ref.shape, 1) - bias_ref.shape[1]
    bias_ref[...] = jnp.where(old_pos >= -seen_tokens, 0.0, floor_value)
    for key_head in range(key_heads):
        queries = stacked_queries(query_ref, key_head, group_width)
        scores = scaled_scores(queries, key_ref[:, head_columns(key_head)])
        score_ref[key_head] = jnp.where(visible, scores, floor_value)
    for load in loads[3:]:
        load.wait()


def weigh_kernel(query_ref, score_ref, bias_ref, old_key_ref, prob_ref, scale_ref):
    row_count = query_ref.shape[0]
    group_width = score_ref.shape[1] // row_count
    bias = jnp.concatenate([bias_ref[...]] * group_width, axis=0)
    for key_head in range(score_ref.shape[0]):
        queries = stacked_queries(query_ref, key_head, group_width)
        old_scores = scaled_scores(queries, old_key_ref[:, head_columns(key_head)]) + bias
        masked = jnp.concatenate([old_scores, score_ref[key_head]], axis=1)
        row_max = jnp.max(masked, axis=-1, keepdims=True)
        probs = jnp.exp(masked - row_max)
        denominator = jnp.sum(probs, axis=-1, keepdims=True)
        prob_ref[key_head] = probs.astype(jnp.bfloat16)
        scale_ref[key_head] = jnp.broadcast_to(1.0 / denominator, scale_ref.shape[1:])


def combine_kernel(prob_ref, scale_ref, value_ref, old_value_ref, *out_refs):
    whole_ref = out_refs[-1]
    row_count = whole_ref.shape[0]
    group_width = prob_ref.shape[1] // row_count
    for key_head in range(prob_ref.shape[0]):
        columns = head_columns(key_head)
        values = jnp.concatenate([old_value_ref[:, columns], value_ref[:, columns]], axis=0)
        combined = jnp.dot(prob_ref[key_head], values, preferred_element_type=jnp.float32)
        combined = (combined * scale_ref[key_head]).astype(jnp.bfloat16)
        for member in range(group_width):
            rows = slice(member * row_count, (member + 1) * row_count)
            whole_ref[:, head_columns(key_head * group_width + member)] = combined[rows]
    if len(out_refs) > 1:
        head_index = lax.axis_index("head")
        for out_ref, flips in zip(out_refs[:2], owner_flips, strict=True):
            own_rows = out_ref.shape[0] // len(flips)
            for at, flip in enumerate(flips):
                first = pl.multiple_of((head_index ^ flip) * own_rows, own_rows)
                out_ref[at * own_rows : (at + 1) * own_rows] = whole_ref[pl.ds(first, own_rows), :]


def attend(queries, keys, values, prefix, turned_weight, reach, in_halves):
    row_count = queries.shape[0]
    key_heads = keys.shape[1] // HEAD_SIZE
    stacked_rows = queries.shape[1] // (key_heads * HEAD_SIZE) * row_count
    params = pltpu.CompilerParams(vmem_limit_bytes=vmem_bytes)
    old_keys = earlier_sections(keys, reach)
    old_values = earlier_sections(values, reach)
    like = lambda array: jax.ShapeDtypeStruct(array.shape, array.dtype)
    own_queries, own_values, weight, scores, bias = pl.pallas_call(
        own_kernel,
        out_shape=(
            like(queries),
            like(values),
            like(turned_weight),
            jax.ShapeDtypeStruct((key_heads, stacked_rows, row_count), jnp.float32),
            jax.ShapeDtypeStruct((row_count, reach * row_count), jnp.float32),
        ),
        in_specs=[in_hbm] * 5,
        out_specs=(in_vmem,) * 5,
        scratch_shapes=[
            pltpu.VMEM(keys.shape, keys.dtype),
            pltpu.SMEM(prefix.shape, prefix.dtype),
            pltpu.SemaphoreType.DMA((5,)),
        ],
        compiler_params=params,
        cost_estimate=no_cost,
        name="own_scores",
    )(*(pltpu.with_memory_space_constraint(array, pltpu.HBM) for array in (prefix, queries, keys, values, turned_weight)))
    half = jax.ShapeDtypeStruct((row_count // 2, queries.shape[1]), queries.dtype)
    probs, scales = pl.pallas_call(
        weigh_kernel,
        out_shape=(
            jax.ShapeDtypeStruct(
                (key_heads, stacked_rows, (reach + 1) * row_count), jnp.bfloat16
            ),
            jax.ShapeDtypeStruct((key_heads, stacked_rows, HEAD_SIZE), jnp.float32),
        ),
        in_specs=[in_vmem] * 4,
        out_specs=(in_vmem,) * 2,
        compiler_params=params,
        cost_estimate=no_cost,
        name="weigh",
    )(own_queries, scores, bias, old_keys)
    attention = pl.pallas_call(
        combine_kernel,
        out_shape=(half, half) if in_halves else like(queries),
        in_specs=[in_vmem] * 4,
        out_specs=(in_vmem, in_vmem) if in_halves else in_vmem,
        scratch_shapes=[pltpu.VMEM(queries.shape, queries.dtype)] if in_halves else [],
        compiler_params=params,
        cost_estimate=no_cost,
        name="attend",
    )(probs, scales, own_values, old_values)
    return attention, weight


def project_kernel(counts, *refs):
    chunks = []
    for count in counts:
        chunk, refs = refs[:count], refs[count:]
        chunks.append(chunk if count == 2 else [chunk[0].at[0], chunk[0].at[1]])
    weight_refs, sent_ref, kept_ref = refs[:2], *refs[-2:]
    product = sum(
        lax.dot_general(
            jnp.concatenate([chunk[at][...] for chunk in chunks], axis=0),
            weight_ref[...],
            (((1,), (1,)), ((), ())),
            preferred_element_type=jnp.float32,
        )
        for at, weight_ref in enumerate(weight_refs)
    )
    rows = sent_ref.shape[1]
    for at in range(len(chunks)):
        first = 2 * rows * at
        sent_ref[at] = product[first : first + rows].astype(jnp.bfloat16)
        kept_ref[at] = product[first + rows : first + 2 * rows]


def project(chunks, weights, earlier):
    shape = (len(chunks), chunks[0][0].shape[-2] // 2, weights[0].shape[0])
    given = [array for chunk in chunks for array in chunk] + list(weights)
    return pl.pallas_call(
        functools.partial(project_kernel, [len(chunk) for chunk in chunks]),
        out_shape=(
            jax.ShapeDtypeStruct(shape, jnp.bfloat16),
            jax.ShapeDtypeStruct(shape, jnp.float32),
        ),
        in_specs=[in_vmem] * len(given) + [anywhere] * len(earlier),
        out_specs=(in_vmem, in_vmem),
        compiler_params=pltpu.CompilerParams(vmem_limit_bytes=vmem_bytes),
        cost_estimate=project_cost,
        name="project",
    )(*given, *earlier)


def stack_kernel(own_ref, other_ref, _, out_ref):
    out_ref[0] = own_ref[...]
    out_ref[1] = other_ref[...]


def stacked_after(own, other, earlier):
    return pl.pallas_call(
        stack_kernel,
        out_shape=jax.ShapeDtypeStruct((2, *own.shape), own.dtype),
        in_specs=[in_vmem, in_vmem, anywhere],
        out_specs=in_vmem,
        compiler_params=pltpu.CompilerParams(vmem_limit_bytes=vmem_bytes),
        cost_estimate=no_cost,
        name="stack",
    )(own, other, earlier)


def finish_kernel(half_ref, arrived_ref, _, out_ref):
    out_ref[...] = (half_ref[...] + arrived_ref[...].astype(jnp.float32)).astype(out_ref.dtype)


def finish_after(half, arrived, earlier):
    return pl.pallas_call(
        finish_kernel,
        out_shape=jax.ShapeDtypeStruct(half.shape, jnp.bfloat16),
        in_specs=[in_vmem, in_vmem, anywhere],
        out_specs=in_vmem,
        compiler_params=pltpu.CompilerParams(vmem_limit_bytes=vmem_bytes),
        cost_estimate=no_cost,
        name="finish",
    )(half, arrived, earlier)


def squares_kernel(has_earlier, *refs):
    *piece_refs, out_ref = refs
    total = piece_refs.pop()[:, :1] if has_earlier else 0.0
    for piece_ref in piece_refs:
        piece = piece_ref[...].astype(jnp.float32)
        total = total + jnp.sum(piece * piece, axis=-1, keepdims=True)
    out_ref[...] = jnp.broadcast_to(total, out_ref.shape)


def squares(pieces, earlier):
    given = list(pieces) if earlier is None else [*pieces, earlier]
    return pl.pallas_call(
        functools.partial(squares_kernel, earlier is not None),
        out_shape=jax.ShapeDtypeStruct((pieces[0].shape[0], HEAD_SIZE), jnp.float32),
        in_specs=[in_vmem] * len(given),
        out_specs=in_vmem,
        compiler_params=pltpu.CompilerParams(vmem_limit_bytes=vmem_bytes),
        cost_estimate=no_cost,
        name="squares",
    )(*given)


def norm_kernel(count, *refs):
    piece_refs = refs[:count]
    squares_ref, residual_ref, gain_ref, out_ref, piece_ref = refs[count:]
    width = piece_ref.shape[2]
    for at, moved_ref in enumerate(piece_refs):
        piece_ref[at] = moved_ref[...].astype(jnp.float32)
    last = piece_ref[last_flip(count)]
    square = squares_ref[:, :1] + jnp.sum(last * last, axis=-1, keepdims=True)
    scale = lax.rsqrt(square / (count * width) + norm_eps)
    section_index = lax.axis_index("section")
    for at in range(count):
        place = slice(at * width, (at + 1) * width)
        normed = piece_ref[section_index ^ at] * scale * gain_ref[:, place]
        out_ref[:, place] = (residual_ref[:, place].astype(jnp.float32) + normed).astype(jnp.bfloat16)


def last_flip(section_total):
    return section_flips(section_total)[-1][-1]


def section_flips(section_total):
    return [[0], list(range(1, section_total - 1)), [section_total - 1]]


def norm(pieces, residual, post_gain):
    early = None
    for group in section_flips(len(pieces))[:-1]:
        early = squares([pieces[flip] for flip in group], early)
    return pl.pallas_call(
        functools.partial(norm_kernel, len(pieces)),
        out_shape=jax.ShapeDtypeStruct(residual.shape, jnp.bfloat16),
        in_specs=[in_vmem] * (len(pieces) + 3),
        out_specs=in_vmem,
        scratch_shapes=[pltpu.VMEM((len(pieces), *pieces[0].shape), jnp.float32)],
        compiler_params=pltpu.CompilerParams(vmem_limit_bytes=vmem_bytes),
        cost_estimate=no_cost,
        name="norm",
    )(*pieces, early, residual, post_gain[None, :])


def local(queries, token_key_rows, token_value_rows, residual, prefix, out_weight, post_gain):
    own_rows = residual.shape[0]
    section_total = lax.axis_size("section")
    head_total = lax.axis_size("head")
    reach = 3 * section_total // 8
    in_halves = (
        2 < section_total <= most_paired and is_power(section_total) and head_total == 4
    )
    turned = out_weight.T
    attention, turned_weight = attend(
        queries, token_key_rows, token_value_rows, prefix, turned, reach, in_halves
    )
    if in_halves:
        weights = [turned_weight, exchanged(turned, "head", 1)]
        sent, kept = attention
        whole = jnp.stack([kept, exchanged(sent, "head", 1)])
        gathered = {0: [whole], 1: [exchanged(whole, "section", 1)]}
        for flip in range(2, section_total):
            if is_power(flip):
                gathered[flip] = [exchanged(kept, "section", flip), crossed(sent, flip)]
        sent, halves, arrivals = None, [], []
        groups = section_flips(section_total)
        for group in groups:
            for flip in group:
                if flip not in gathered:
                    lowest = flip & -flip
                    [source] = gathered[flip ^ lowest]
                    gathered[flip] = [exchanged(source, "section", lowest)]
            chunks = [gathered[flip] for flip in group]
            sent, half = project(chunks, weights, [] if sent is None else [sent])
            halves.append(half)
            arrivals.append(exchanged(sent, "head", 2))
            if group is groups[0]:
                for flip in range(2, section_total):
                    if is_power(flip):
                        gathered[flip] = [stacked_after(*gathered[flip], sent)]
        ready = {
            flip: (half[at], arrived[at])
            for group, half, arrived in zip(groups, halves, arrivals, strict=True)
            for at, flip in enumerate(group)
        }
        totals = {
            flip: half + arrived.astype(jnp.float32)
            for flip, (half, arrived) in ready.items()
            if flip != 1
        }
        sends = {flip: totals[flip].astype(jnp.bfloat16) for flip in range(2, section_total)}
        sends[1] = finish_after(*ready[1], sends[2])
        pieces = [totals[0]] + [
            exchanged(sends[flip], "section", flip) for flip in range(1, section_total)
        ]
        return norm(pieces, residual, post_gain)
    gathered = lax.all_gather(attention, "section", axis=0, tiled=True)
    product = jnp.dot(gathered, turned_weight.T, preferred_element_type=jnp.float32)
    product = product.astype(jnp.bfloat16).reshape(-1, head_total, own_rows, product.shape[-1])
    sums = lax.psum_scatter(product, "head", scatter_dimension=1, tiled=False)
    pieces = lax.all_to_all(sums, "section", 0, 0)
    summed = jnp.transpose(pieces, (1, 0, 2)).reshape(own_rows, -1).astype(jnp.float32)
    mean_square = jnp.mean(summed * summed, axis=-1, keepdims=True)
    normed = summed * lax.rsqrt(mean_square + norm_eps) * post_gain[None, :]
    return (residual.astype(jnp.float32) + normed).astype(jnp.bfloat16)


def solution(mesh):
    placed = (
        P(("groups", "section"), "head"),
        P(("groups", "section"), "head"),
        P(("groups", "section"), "head"),
        P(("groups", "section", "head"), None),
        P("groups"),
        P("head", "section"),
        P(),
    )
    return jax.shard_map(
        local,
        mesh=mesh,
        in_specs=placed,
        out_specs=P(("groups", "section", "head"), None),
        check_vma=False,
    )
```

```python
import functools

import jax
import jax.numpy as jnp
from jax import lax
from jax.experimental import pallas as pl
from jax.experimental.pallas import tpu as pltpu
from jax.sharding import PartitionSpec as P

HEAD_SIZE = 128


score_scale = 168.0 ** (-0.5)
floor_value = -1e30
norm_eps = 1e-06
vmem_bytes = 24 * 2**20
owner_flips = ((3, 1), (2, 0))
most_paired = 8

in_vmem = pl.BlockSpec(memory_space=pltpu.VMEM)
in_smem = pl.BlockSpec(memory_space=pltpu.SMEM)
in_hbm = pl.BlockSpec(memory_space=pltpu.HBM)
anywhere = pl.BlockSpec(memory_space=pl.ANY)


no_cost = pl.CostEstimate(flops=0, transcendentals=0, bytes_accessed=0)
project_cost = pl.CostEstimate(flops=3 * 10**9, transcendentals=0, bytes_accessed=0)


def is_power(count):
    return count & (count - 1) == 0


def rotated(value, axis, steps):
    count = lax.axis_size(axis)
    return lax.ppermute(value, axis, [(at, (at + steps) % count) for at in range(count)])


def exchanged(value, axis, flip):
    count = lax.axis_size(axis)
    return lax.ppermute(value, axis, [(at, at ^ flip) for at in range(count)])


def crossed(value, flip):
    sections, heads = lax.axis_size("section"), lax.axis_size("head")
    pairs = [
        (section * heads + head, (section ^ flip) * heads + (head ^ 1))
        for section in range(sections)
        for head in range(heads)
    ]
    return lax.ppermute(value, ("section", "head"), pairs)


def earlier_sections(own_rows, reach):
    held = own_rows[None]
    stride = 1
    while stride <= reach:
        moved_count = min(stride, reach + 1 - stride)
        held = jnp.concatenate([held, rotated(held[:moved_count], "section", stride)], axis=0)
        stride = stride * 2
    return held[:0:-1].reshape(reach * own_rows.shape[0], own_rows.shape[1])


def head_columns(head):
    return slice(head * HEAD_SIZE, (head + 1) * HEAD_SIZE)


def stacked_queries(query_ref, key_head, group_width):
    first = key_head * group_width
    return jnp.concatenate(
        [query_ref[:, head_columns(head)] for head in range(first, first + group_width)], axis=0
    )


def scaled_scores(queries, keys):
    product = lax.dot_general(
        queries, keys, (((1,), (1,)), ((), ())), preferred_element_type=jnp.float32
    )
    return product * score_scale


def own_kernel(
    prefix_in,
    query_in,
    key_in,
    value_in,
    weight_in,
    query_ref,
    value_ref,
    weight_ref,
    score_ref,
    bias_ref,
    key_ref,
    prefix_ref,
    sems,
):
    loads = [
        pltpu.make_async_copy(source, target, sems.at[at])
        for at, (source, target) in enumerate(
            (
                (prefix_in, prefix_ref),
                (query_in, query_ref),
                (key_in, key_ref),
                (value_in, value_ref),
                (weight_in, weight_ref),
            )
        )
    ]
    for load in loads:
        load.start()
    row_count = query_ref.shape[0]
    key_heads = key_ref.shape[1] // HEAD_SIZE
    group_width = query_ref.shape[1] // (key_heads * HEAD_SIZE)
    shape = (row_count, row_count)
    visible = lax.broadcasted_iota(jnp.int32, shape, 1) <= lax.broadcasted_iota(jnp.int32, shape, 0)
    visible = jnp.concatenate([visible] * group_width, axis=0)
    for load in loads[:3]:
        load.wait()
    section_index = lax.axis_index("section")
    seen_tokens = jnp.minimum(section_index * row_count, prefix_ref[section_index])
    old_pos = lax.broadcasted_iota(jnp.int32, bias_ref.shape, 1) - bias_ref.shape[1]
    bias_ref[...] = jnp.where(old_pos >= -seen_tokens, 0.0, floor_value)
    for key_head in range(key_heads):
        queries = stacked_queries(query_ref, key_head, group_width)
        scores = scaled_scores(queries, key_ref[:, head_columns(key_head)])
        score_ref[key_head] = jnp.where(visible, scores, floor_value)
    for load in loads[3:]:
        load.wait()


def weigh_kernel(query_ref, score_ref, bias_ref, old_key_ref, prob_ref, scale_ref):
    row_count = query_ref.shape[0]
    group_width = score_ref.shape[1] // row_count
    bias = jnp.concatenate([bias_ref[...]] * group_width, axis=0)
    for key_head in range(score_ref.shape[0]):
        queries = stacked_queries(query_ref, key_head, group_width)
        old_scores = scaled_scores(queries, old_key_ref[:, head_columns(key_head)]) + bias
        masked = jnp.concatenate([old_scores, score_ref[key_head]], axis=1)
        row_max = jnp.max(masked, axis=-1, keepdims=True)
        probs = jnp.exp(masked - row_max)
        denominator = jnp.sum(probs, axis=-1, keepdims=True)
        prob_ref[key_head] = probs.astype(jnp.bfloat16)
        scale_ref[key_head] = jnp.broadcast_to(1.0 / denominator, scale_ref.shape[1:])


def combine_kernel(prob_ref, scale_ref, value_ref, old_value_ref, *out_refs):
    whole_ref = out_refs[-1]
    row_count = whole_ref.shape[0]
    group_width = prob_ref.shape[1] // row_count
    for key_head in range(prob_ref.shape[0]):
        columns = head_columns(key_head)
        values = jnp.concatenate([old_value_ref[:, columns], value_ref[:, columns]], axis=0)
        combined = jnp.dot(prob_ref[key_head], values, preferred_element_type=jnp.float32)
        combined = (combined * scale_ref[key_head]).astype(jnp.bfloat16)
        for member in range(group_width):
            rows = slice(member * row_count, (member + 1) * row_count)
            whole_ref[:, head_columns(key_head * group_width + member)] = combined[rows]
    if len(out_refs) > 1:
        head_index = lax.axis_index("head")
        for out_ref, flips in zip(out_refs[:2], owner_flips, strict=True):
            own_rows = out_ref.shape[0] // len(flips)
            for at, flip in enumerate(flips):
                first = pl.multiple_of((head_index ^ flip) * own_rows, own_rows)
                out_ref[at * own_rows : (at + 1) * own_rows] = whole_ref[pl.ds(first, own_rows), :]


def attend(queries, keys, values, prefix, turned_weight, reach, in_halves):
    row_count = queries.shape[0]
    key_heads = keys.shape[1] // HEAD_SIZE
    stacked_rows = queries.shape[1] // (key_heads * HEAD_SIZE) * row_count
    params = pltpu.CompilerParams(vmem_limit_bytes=vmem_bytes)
    old_keys = earlier_sections(keys, reach)
    old_values = earlier_sections(values, reach)
    like = lambda array: jax.ShapeDtypeStruct(array.shape, array.dtype)
    own_queries, own_values, weight, scores, bias = pl.pallas_call(
        own_kernel,
        out_shape=(
            like(queries),
            like(values),
            like(turned_weight),
            jax.ShapeDtypeStruct((key_heads, stacked_rows, row_count), jnp.float32),
            jax.ShapeDtypeStruct((row_count, reach * row_count), jnp.float32),
        ),
        in_specs=[in_hbm] * 5,
        out_specs=(in_vmem,) * 5,
        scratch_shapes=[
            pltpu.VMEM(keys.shape, keys.dtype),
            pltpu.SMEM(prefix.shape, prefix.dtype),
            pltpu.SemaphoreType.DMA((5,)),
        ],
        compiler_params=params,
        cost_estimate=no_cost,
        name="own_scores",
    )(*(pltpu.with_memory_space_constraint(array, pltpu.HBM) for array in (prefix, queries, keys, values, turned_weight)))
    half = jax.ShapeDtypeStruct((row_count // 2, queries.shape[1]), queries.dtype)
    probs, scales = pl.pallas_call(
        weigh_kernel,
        out_shape=(
            jax.ShapeDtypeStruct(
                (key_heads, stacked_rows, (reach + 1) * row_count), jnp.bfloat16
            ),
            jax.ShapeDtypeStruct((key_heads, stacked_rows, HEAD_SIZE), jnp.float32),
        ),
        in_specs=[in_vmem] * 4,
        out_specs=(in_vmem,) * 2,
        compiler_params=params,
        cost_estimate=no_cost,
        name="weigh",
    )(own_queries, scores, bias, old_keys)
    attention = pl.pallas_call(
        combine_kernel,
        out_shape=(half, half) if in_halves else like(queries),
        in_specs=[in_vmem] * 4,
        out_specs=(in_vmem, in_vmem) if in_halves else in_vmem,
        scratch_shapes=[pltpu.VMEM(queries.shape, queries.dtype)] if in_halves else [],
        compiler_params=params,
        cost_estimate=no_cost,
        name="attend",
    )(probs, scales, own_values, old_values)
    return attention, weight


def project_kernel(counts, *refs):
    chunks = []
    for count in counts:
        chunk, refs = refs[:count], refs[count:]
        chunks.append(chunk if count == 2 else [chunk[0].at[0], chunk[0].at[1]])
    weight_refs, sent_ref, kept_ref = refs[:2], *refs[-2:]
    product = sum(
        lax.dot_general(
            jnp.concatenate([chunk[at][...] for chunk in chunks], axis=0),
            weight_ref[...],
            (((1,), (1,)), ((), ())),
            preferred_element_type=jnp.float32,
        )
        for at, weight_ref in enumerate(weight_refs)
    )
    rows = sent_ref.shape[1]
    for at in range(len(chunks)):
        first = 2 * rows * at
        sent_ref[at] = product[first : first + rows].astype(jnp.bfloat16)
        kept_ref[at] = product[first + rows : first + 2 * rows]


def project(chunks, weights, earlier):
    shape = (len(chunks), chunks[0][0].shape[-2] // 2, weights[0].shape[0])
    given = [array for chunk in chunks for array in chunk] + list(weights)
    return pl.pallas_call(
        functools.partial(project_kernel, [len(chunk) for chunk in chunks]),
        out_shape=(
            jax.ShapeDtypeStruct(shape, jnp.bfloat16),
            jax.ShapeDtypeStruct(shape, jnp.float32),
        ),
        in_specs=[in_vmem] * len(given) + [anywhere] * len(earlier),
        out_specs=(in_vmem, in_vmem),
        compiler_params=pltpu.CompilerParams(vmem_limit_bytes=vmem_bytes),
        cost_estimate=project_cost,
        name="project",
    )(*given, *earlier)


def stack_kernel(own_ref, other_ref, _, out_ref):
    out_ref[0] = own_ref[...]
    out_ref[1] = other_ref[...]


def stacked_after(own, other, earlier):
    return pl.pallas_call(
        stack_kernel,
        out_shape=jax.ShapeDtypeStruct((2, *own.shape), own.dtype),
        in_specs=[in_vmem, in_vmem, anywhere],
        out_specs=in_vmem,
        compiler_params=pltpu.CompilerParams(vmem_limit_bytes=vmem_bytes),
        cost_estimate=no_cost,
        name="stack",
    )(own, other, earlier)


def finish_kernel(half_ref, arrived_ref, _, out_ref):
    out_ref[...] = (half_ref[...] + arrived_ref[...].astype(jnp.float32)).astype(out_ref.dtype)


def finish_after(half, arrived, earlier):
    return pl.pallas_call(
        finish_kernel,
        out_shape=jax.ShapeDtypeStruct(half.shape, jnp.bfloat16),
        in_specs=[in_vmem, in_vmem, anywhere],
        out_specs=in_vmem,
        compiler_params=pltpu.CompilerParams(vmem_limit_bytes=vmem_bytes),
        cost_estimate=no_cost,
        name="finish",
    )(half, arrived, earlier)


def squares_kernel(has_earlier, *refs):
    *piece_refs, out_ref = refs
    total = piece_refs.pop()[:, :1] if has_earlier else 0.0
    for piece_ref in piece_refs:
        piece = piece_ref[...].astype(jnp.float32)
        total = total + jnp.sum(piece * piece, axis=-1, keepdims=True)
    out_ref[...] = jnp.broadcast_to(total, out_ref.shape)


def squares(pieces, earlier):
    given = list(pieces) if earlier is None else [*pieces, earlier]
    return pl.pallas_call(
        functools.partial(squares_kernel, earlier is not None),
        out_shape=jax.ShapeDtypeStruct((pieces[0].shape[0], HEAD_SIZE), jnp.float32),
        in_specs=[in_vmem] * len(given),
        out_specs=in_vmem,
        compiler_params=pltpu.CompilerParams(vmem_limit_bytes=vmem_bytes),
        cost_estimate=no_cost,
        name="squares",
    )(*given)


def norm_kernel(count, *refs):
    piece_refs = refs[:count]
    squares_ref, residual_ref, gain_ref, out_ref, piece_ref, made_ref, sems = refs[count:]
    width = piece_ref.shape[2]
    for at, moved_ref in enumerate(piece_refs):
        piece_ref[at] = moved_ref[...].astype(jnp.float32)
    last = piece_ref[last_flip(count)]
    square = squares_ref[:, :1] + jnp.sum(last * last, axis=-1, keepdims=True)
    scale = lax.rsqrt(square / (count * width) + norm_eps)
    section_index = lax.axis_index("section")
    steps = sems.shape[0]
    together = count // steps
    stores = []
    for step in range(steps):
        first = step * together
        place = slice(first * width, (first + together) * width)
        wide = [piece_ref[section_index ^ at] for at in range(first, first + together)]
        normed = jnp.concatenate(wide, axis=1) * scale * gain_ref[:, place]
        made_ref[:, place] = (residual_ref[:, place].astype(jnp.float32) + normed).astype(jnp.bfloat16)
        stores.append(
            pltpu.make_async_copy(made_ref.at[:, place], out_ref.at[:, place], sems.at[step])
        )
        stores[-1].start()
    for store in stores:
        store.wait()


def last_flip(section_total):
    return section_flips(section_total)[-1][-1]


def section_flips(section_total):
    return [[0], list(range(1, section_total - 1)), [section_total - 1]]


def norm(pieces, residual, post_gain):
    early = None
    for group in section_flips(len(pieces))[:-1]:
        early = squares([pieces[flip] for flip in group], early)
    count, width = len(pieces), pieces[0].shape[1]
    steps = 2 if count * width % (2 * HEAD_SIZE) == 0 else 1
    return pl.pallas_call(
        functools.partial(norm_kernel, count),
        out_shape=jax.ShapeDtypeStruct(residual.shape, jnp.bfloat16),
        in_specs=[in_vmem] * (count + 3),
        out_specs=in_hbm,
        scratch_shapes=[
            pltpu.VMEM((count, *pieces[0].shape), jnp.float32),
            pltpu.VMEM(residual.shape, jnp.bfloat16),
            pltpu.SemaphoreType.DMA((steps,)),
        ],
        compiler_params=pltpu.CompilerParams(vmem_limit_bytes=vmem_bytes),
        cost_estimate=no_cost,
        name="norm",
    )(*pieces, early, residual, post_gain[None, :])


def local(queries, token_key_rows, token_value_rows, residual, prefix, out_weight, post_gain):
    own_rows = residual.shape[0]
    section_total = lax.axis_size("section")
    head_total = lax.axis_size("head")
    reach = 3 * section_total // 8
    in_halves = (
        2 < section_total <= most_paired and is_power(section_total) and head_total == 4
    )
    turned = out_weight.T
    attention, turned_weight = attend(
        queries, token_key_rows, token_value_rows, prefix, turned, reach, in_halves
    )
    if in_halves:
        weights = [turned_weight, exchanged(turned, "head", 1)]
        sent, kept = attention
        whole = jnp.stack([kept, exchanged(sent, "head", 1)])
        gathered = {0: [whole], 1: [exchanged(whole, "section", 1)]}
        for flip in range(2, section_total):
            if is_power(flip):
                gathered[flip] = [exchanged(kept, "section", flip), crossed(sent, flip)]
        sent, halves, arrivals = None, [], []
        groups = section_flips(section_total)
        for group in groups:
            for flip in group:
                if flip not in gathered:
                    lowest = flip & -flip
                    [source] = gathered[flip ^ lowest]
                    gathered[flip] = [exchanged(source, "section", lowest)]
            chunks = [gathered[flip] for flip in group]
            sent, half = project(chunks, weights, [] if sent is None else [sent])
            halves.append(half)
            arrivals.append(exchanged(sent, "head", 2))
            if group is groups[0]:
                for flip in range(2, section_total):
                    if is_power(flip):
                        gathered[flip] = [stacked_after(*gathered[flip], sent)]
        ready = {
            flip: (half[at], arrived[at])
            for group, half, arrived in zip(groups, halves, arrivals, strict=True)
            for at, flip in enumerate(group)
        }
        totals = {
            flip: half + arrived.astype(jnp.float32)
            for flip, (half, arrived) in ready.items()
            if flip != 1
        }
        sends = {flip: totals[flip].astype(jnp.bfloat16) for flip in range(2, section_total)}
        sends[1] = finish_after(*ready[1], sends[2])
        pieces = [totals[0]] + [
            exchanged(sends[flip], "section", flip) for flip in range(1, section_total)
        ]
        return norm(pieces, residual, post_gain)
    gathered = lax.all_gather(attention, "section", axis=0, tiled=True)
    product = jnp.dot(gathered, turned_weight.T, preferred_element_type=jnp.float32)
    product = product.astype(jnp.bfloat16).reshape(-1, head_total, own_rows, product.shape[-1])
    sums = lax.psum_scatter(product, "head", scatter_dimension=1, tiled=False)
    pieces = lax.all_to_all(sums, "section", 0, 0)
    summed = jnp.transpose(pieces, (1, 0, 2)).reshape(own_rows, -1).astype(jnp.float32)
    mean_square = jnp.mean(summed * summed, axis=-1, keepdims=True)
    normed = summed * lax.rsqrt(mean_square + norm_eps) * post_gain[None, :]
    return (residual.astype(jnp.float32) + normed).astype(jnp.bfloat16)


def solution(mesh):
    placed = (
        P(("groups", "section"), "head"),
        P(("groups", "section"), "head"),
        P(("groups", "section"), "head"),
        P(("groups", "section", "head"), None),
        P("groups"),
        P("head", "section"),
        P(),
    )
    return jax.shard_map(
        local,
        mesh=mesh,
        in_specs=placed,
        out_specs=P(("groups", "section", "head"), None),
        check_vma=False,
    )
```

```python
import functools

import jax
import jax.numpy as jnp
from jax import lax
from jax.experimental import pallas as pl
from jax.experimental.pallas import tpu as pltpu
from jax.sharding import PartitionSpec as P

HEAD_SIZE = 128


score_scale = 168.0 ** (-0.5)
floor_value = -1e30
norm_eps = 1e-06
vmem_bytes = 24 * 2**20
owner_flips = ((3, 1), (2, 0))
most_paired = 8

in_vmem = pl.BlockSpec(memory_space=pltpu.VMEM)
in_smem = pl.BlockSpec(memory_space=pltpu.SMEM)
in_hbm = pl.BlockSpec(memory_space=pltpu.HBM)
anywhere = pl.BlockSpec(memory_space=pl.ANY)


no_cost = pl.CostEstimate(flops=0, transcendentals=0, bytes_accessed=0)
project_cost = pl.CostEstimate(flops=3 * 10**9, transcendentals=0, bytes_accessed=0)


def is_power(count):
    return count & (count - 1) == 0


def rotated(value, axis, steps):
    count = lax.axis_size(axis)
    return lax.ppermute(value, axis, [(at, (at + steps) % count) for at in range(count)])


def exchanged(value, axis, flip):
    count = lax.axis_size(axis)
    return lax.ppermute(value, axis, [(at, at ^ flip) for at in range(count)])


def crossed(value, flip):
    sections, heads = lax.axis_size("section"), lax.axis_size("head")
    pairs = [
        (section * heads + head, (section ^ flip) * heads + (head ^ 1))
        for section in range(sections)
        for head in range(heads)
    ]
    return lax.ppermute(value, ("section", "head"), pairs)


def earlier_sections(own_rows, reach):
    held = own_rows[None]
    stride = 1
    while stride <= reach:
        moved_count = min(stride, reach + 1 - stride)
        held = jnp.concatenate([held, rotated(held[:moved_count], "section", stride)], axis=0)
        stride = stride * 2
    return held[:0:-1].reshape(reach * own_rows.shape[0], own_rows.shape[1])


def head_columns(head):
    return slice(head * HEAD_SIZE, (head + 1) * HEAD_SIZE)


def stacked_queries(query_ref, key_head, group_width):
    first = key_head * group_width
    return jnp.concatenate(
        [query_ref[:, head_columns(head)] for head in range(first, first + group_width)], axis=0
    )


def scaled_scores(queries, keys):
    product = lax.dot_general(
        queries, keys, (((1,), (1,)), ((), ())), preferred_element_type=jnp.float32
    )
    return product * score_scale


def own_kernel(
    prefix_in,
    query_in,
    key_in,
    value_in,
    weight_in,
    query_ref,
    value_ref,
    weight_ref,
    score_ref,
    bias_ref,
    key_ref,
    prefix_ref,
    sems,
):
    loads = [
        pltpu.make_async_copy(source, target, sems.at[at])
        for at, (source, target) in enumerate(
            (
                (prefix_in, prefix_ref),
                (query_in, query_ref),
                (key_in, key_ref),
                (value_in, value_ref),
                (weight_in, weight_ref),
            )
        )
    ]
    for load in loads:
        load.start()
    row_count = query_ref.shape[0]
    key_heads = key_ref.shape[1] // HEAD_SIZE
    group_width = query_ref.shape[1] // (key_heads * HEAD_SIZE)
    shape = (row_count, row_count)
    visible = lax.broadcasted_iota(jnp.int32, shape, 1) <= lax.broadcasted_iota(jnp.int32, shape, 0)
    visible = jnp.concatenate([visible] * group_width, axis=0)
    for load in loads[:3]:
        load.wait()
    section_index = lax.axis_index("section")
    seen_tokens = jnp.minimum(section_index * row_count, prefix_ref[section_index])
    old_pos = lax.broadcasted_iota(jnp.int32, bias_ref.shape, 1) - bias_ref.shape[1]
    bias_ref[...] = jnp.where(old_pos >= -seen_tokens, 0.0, floor_value)
    for key_head in range(key_heads):
        queries = stacked_queries(query_ref, key_head, group_width)
        scores = scaled_scores(queries, key_ref[:, head_columns(key_head)])
        score_ref[key_head] = jnp.where(visible, scores, floor_value)
    for load in loads[3:]:
        load.wait()


def weigh_kernel(query_ref, score_ref, bias_ref, old_key_ref, prob_ref, scale_ref):
    row_count = query_ref.shape[0]
    group_width = score_ref.shape[1] // row_count
    bias = jnp.concatenate([bias_ref[...]] * group_width, axis=0)
    for key_head in range(score_ref.shape[0]):
        queries = stacked_queries(query_ref, key_head, group_width)
        old_scores = scaled_scores(queries, old_key_ref[:, head_columns(key_head)]) + bias
        masked = jnp.concatenate([old_scores, score_ref[key_head]], axis=1)
        row_max = jnp.max(masked, axis=-1, keepdims=True)
        probs = jnp.exp(masked - row_max)
        denominator = jnp.sum(probs, axis=-1, keepdims=True)
        prob_ref[key_head] = probs.astype(jnp.bfloat16)
        scale_ref[key_head] = jnp.broadcast_to(1.0 / denominator, scale_ref.shape[1:])


def combine_kernel(prob_ref, scale_ref, value_ref, old_value_ref, *out_refs):
    whole_ref = out_refs[-1]
    row_count = whole_ref.shape[0]
    group_width = prob_ref.shape[1] // row_count
    for key_head in range(prob_ref.shape[0]):
        columns = head_columns(key_head)
        values = jnp.concatenate([old_value_ref[:, columns], value_ref[:, columns]], axis=0)
        combined = jnp.dot(prob_ref[key_head], values, preferred_element_type=jnp.float32)
        combined = (combined * scale_ref[key_head]).astype(jnp.bfloat16)
        for member in range(group_width):
            rows = slice(member * row_count, (member + 1) * row_count)
            whole_ref[:, head_columns(key_head * group_width + member)] = combined[rows]
    if len(out_refs) > 1:
        head_index = lax.axis_index("head")
        for out_ref, flips in zip(out_refs[:2], owner_flips, strict=True):
            own_rows = out_ref.shape[0] // len(flips)
            for at, flip in enumerate(flips):
                first = pl.multiple_of((head_index ^ flip) * own_rows, own_rows)
                out_ref[at * own_rows : (at + 1) * own_rows] = whole_ref[pl.ds(first, own_rows), :]


def attend(queries, keys, values, prefix, turned_weight, reach, in_halves):
    row_count = queries.shape[0]
    key_heads = keys.shape[1] // HEAD_SIZE
    stacked_rows = queries.shape[1] // (key_heads * HEAD_SIZE) * row_count
    params = pltpu.CompilerParams(vmem_limit_bytes=vmem_bytes)
    old_keys = earlier_sections(keys, reach)
    old_values = earlier_sections(values, reach)
    like = lambda array: jax.ShapeDtypeStruct(array.shape, array.dtype)
    own_queries, own_values, weight, scores, bias = pl.pallas_call(
        own_kernel,
        out_shape=(
            like(queries),
            like(values),
            like(turned_weight),
            jax.ShapeDtypeStruct((key_heads, stacked_rows, row_count), jnp.float32),
            jax.ShapeDtypeStruct((row_count, reach * row_count), jnp.float32),
        ),
        in_specs=[in_hbm] * 5,
        out_specs=(in_vmem,) * 5,
        scratch_shapes=[
            pltpu.VMEM(keys.shape, keys.dtype),
            pltpu.SMEM(prefix.shape, prefix.dtype),
            pltpu.SemaphoreType.DMA((5,)),
        ],
        compiler_params=params,
        cost_estimate=no_cost,
        name="own_scores",
    )(*(pltpu.with_memory_space_constraint(array, pltpu.HBM) for array in (prefix, queries, keys, values, turned_weight)))
    half = jax.ShapeDtypeStruct((row_count // 2, queries.shape[1]), queries.dtype)
    probs, scales = pl.pallas_call(
        weigh_kernel,
        out_shape=(
            jax.ShapeDtypeStruct(
                (key_heads, stacked_rows, (reach + 1) * row_count), jnp.bfloat16
            ),
            jax.ShapeDtypeStruct((key_heads, stacked_rows, HEAD_SIZE), jnp.float32),
        ),
        in_specs=[in_vmem] * 4,
        out_specs=(in_vmem,) * 2,
        compiler_params=params,
        cost_estimate=no_cost,
        name="weigh",
    )(own_queries, scores, bias, old_keys)
    attention = pl.pallas_call(
        combine_kernel,
        out_shape=(half, half) if in_halves else like(queries),
        in_specs=[in_vmem] * 4,
        out_specs=(in_vmem, in_vmem) if in_halves else in_vmem,
        scratch_shapes=[pltpu.VMEM(queries.shape, queries.dtype)] if in_halves else [],
        compiler_params=params,
        cost_estimate=no_cost,
        name="attend",
    )(probs, scales, own_values, old_values)
    return attention, weight


def project_kernel(counts, *refs):
    chunks = []
    for count in counts:
        chunk, refs = refs[:count], refs[count:]
        chunks.append(chunk if count == 2 else [chunk[0].at[0], chunk[0].at[1]])
    weight_refs, sent_ref, kept_ref = refs[:2], *refs[-2:]
    product = sum(
        lax.dot_general(
            jnp.concatenate([chunk[at][...] for chunk in chunks], axis=0),
            weight_ref[...],
            (((1,), (1,)), ((), ())),
            preferred_element_type=jnp.float32,
        )
        for at, weight_ref in enumerate(weight_refs)
    )
    rows = sent_ref.shape[1]
    for at in range(len(chunks)):
        first = 2 * rows * at
        sent_ref[at] = product[first : first + rows].astype(jnp.bfloat16)
        kept_ref[at] = product[first + rows : first + 2 * rows]


def project(chunks, weights, earlier):
    shape = (len(chunks), chunks[0][0].shape[-2] // 2, weights[0].shape[0])
    given = [array for chunk in chunks for array in chunk] + list(weights)
    return pl.pallas_call(
        functools.partial(project_kernel, [len(chunk) for chunk in chunks]),
        out_shape=(
            jax.ShapeDtypeStruct(shape, jnp.bfloat16),
            jax.ShapeDtypeStruct(shape, jnp.float32),
        ),
        in_specs=[in_vmem] * len(given) + [anywhere] * len(earlier),
        out_specs=(in_vmem, in_vmem),
        compiler_params=pltpu.CompilerParams(vmem_limit_bytes=vmem_bytes),
        cost_estimate=project_cost,
        name="project",
    )(*given, *earlier)


def stack_kernel(own_ref, other_ref, _, out_ref):
    out_ref[0] = own_ref[...]
    out_ref[1] = other_ref[...]


def stacked_after(own, other, earlier):
    return pl.pallas_call(
        stack_kernel,
        out_shape=jax.ShapeDtypeStruct((2, *own.shape), own.dtype),
        in_specs=[in_vmem, in_vmem, anywhere],
        out_specs=in_vmem,
        compiler_params=pltpu.CompilerParams(vmem_limit_bytes=vmem_bytes),
        cost_estimate=no_cost,
        name="stack",
    )(own, other, earlier)


def finish_kernel(half_ref, arrived_ref, _, out_ref):
    out_ref[...] = (half_ref[...] + arrived_ref[...].astype(jnp.float32)).astype(out_ref.dtype)


def finish_after(half, arrived, earlier):
    return pl.pallas_call(
        finish_kernel,
        out_shape=jax.ShapeDtypeStruct(half.shape, jnp.bfloat16),
        in_specs=[in_vmem, in_vmem, anywhere],
        out_specs=in_vmem,
        compiler_params=pltpu.CompilerParams(vmem_limit_bytes=vmem_bytes),
        cost_estimate=no_cost,
        name="finish",
    )(half, arrived, earlier)


def squares_kernel(has_earlier, *refs):
    *piece_refs, out_ref = refs
    total = piece_refs.pop()[:, :1] if has_earlier else 0.0
    for piece_ref in piece_refs:
        piece = piece_ref[...].astype(jnp.float32)
        total = total + jnp.sum(piece * piece, axis=-1, keepdims=True)
    out_ref[...] = jnp.broadcast_to(total, out_ref.shape)


def squares(pieces, earlier):
    given = list(pieces) if earlier is None else [*pieces, earlier]
    return pl.pallas_call(
        functools.partial(squares_kernel, earlier is not None),
        out_shape=jax.ShapeDtypeStruct((pieces[0].shape[0], HEAD_SIZE), jnp.float32),
        in_specs=[in_vmem] * len(given),
        out_specs=in_vmem,
        compiler_params=pltpu.CompilerParams(vmem_limit_bytes=vmem_bytes),
        cost_estimate=no_cost,
        name="squares",
    )(*given)


def norm_kernel(count, *refs):
    piece_refs = refs[:count]
    squares_ref, residual_ref, gain_ref, out_ref, piece_ref = refs[count:]
    width = piece_ref.shape[2]
    for at, moved_ref in enumerate(piece_refs):
        piece_ref[at] = moved_ref[...].astype(jnp.float32)
    last = piece_ref[last_flip(count)]
    square = squares_ref[:, :1] + jnp.sum(last * last, axis=-1, keepdims=True)
    scale = lax.rsqrt(square / (count * width) + norm_eps)
    section_index = lax.axis_index("section")
    for at in range(count):
        place = slice(at * width, (at + 1) * width)
        normed = piece_ref[section_index ^ at] * scale * gain_ref[:, place]
        out_ref[:, place] = (residual_ref[:, place].astype(jnp.float32) + normed).astype(jnp.bfloat16)


def last_flip(section_total):
    return section_flips(section_total)[-1][-1]


def section_flips(section_total):
    return [[0], list(range(1, section_total - 1)), [section_total - 1]]


def norm(pieces, residual, post_gain):
    last = last_flip(len(pieces))
    early = squares([piece for flip, piece in enumerate(pieces) if flip != last], None)
    return pl.pallas_call(
        functools.partial(norm_kernel, len(pieces)),
        out_shape=jax.ShapeDtypeStruct(residual.shape, jnp.bfloat16),
        in_specs=[in_vmem] * (len(pieces) + 3),
        out_specs=in_vmem,
        scratch_shapes=[pltpu.VMEM((len(pieces), *pieces[0].shape), jnp.float32)],
        compiler_params=pltpu.CompilerParams(vmem_limit_bytes=vmem_bytes),
        cost_estimate=no_cost,
        name="norm",
    )(*pieces, early, residual, post_gain[None, :])


def local(queries, token_key_rows, token_value_rows, residual, prefix, out_weight, post_gain):
    own_rows = residual.shape[0]
    section_total = lax.axis_size("section")
    head_total = lax.axis_size("head")
    reach = 3 * section_total // 8
    in_halves = (
        2 < section_total <= most_paired and is_power(section_total) and head_total == 4
    )
    turned = out_weight.T
    attention, turned_weight = attend(
        queries, token_key_rows, token_value_rows, prefix, turned, reach, in_halves
    )
    if in_halves:
        weights = [turned_weight, exchanged(turned, "head", 1)]
        sent, kept = attention
        whole = jnp.stack([kept, exchanged(sent, "head", 1)])
        gathered = {0: [whole], 1: [exchanged(whole, "section", 1)]}
        for flip in range(2, section_total):
            if is_power(flip):
                gathered[flip] = [exchanged(kept, "section", flip), crossed(sent, flip)]
        sent, halves, arrivals = None, [], []
        groups = section_flips(section_total)
        for group in groups:
            for flip in group:
                if flip not in gathered:
                    lowest = flip & -flip
                    [source] = gathered[flip ^ lowest]
                    gathered[flip] = [exchanged(source, "section", lowest)]
            chunks = [gathered[flip] for flip in group]
            sent, half = project(chunks, weights, [] if sent is None else [sent])
            halves.append(half)
            arrivals.append(exchanged(sent, "head", 2))
            if group is groups[0]:
                for flip in range(2, section_total):
                    if is_power(flip):
                        gathered[flip] = [stacked_after(*gathered[flip], sent)]
        ready = {
            flip: (half[at], arrived[at])
            for group, half, arrived in zip(groups, halves, arrivals, strict=True)
            for at, flip in enumerate(group)
        }
        totals = {
            flip: half + arrived.astype(jnp.float32)
            for flip, (half, arrived) in ready.items()
            if flip != 1
        }
        sends = {flip: totals[flip].astype(jnp.bfloat16) for flip in range(2, section_total)}
        sends[1] = finish_after(*ready[1], sends[2])
        pieces = [totals[0]] + [
            exchanged(sends[flip], "section", flip) for flip in range(1, section_total)
        ]
        return norm(pieces, residual, post_gain)
    gathered = lax.all_gather(attention, "section", axis=0, tiled=True)
    product = jnp.dot(gathered, turned_weight.T, preferred_element_type=jnp.float32)
    product = product.astype(jnp.bfloat16).reshape(-1, head_total, own_rows, product.shape[-1])
    sums = lax.psum_scatter(product, "head", scatter_dimension=1, tiled=False)
    pieces = lax.all_to_all(sums, "section", 0, 0)
    summed = jnp.transpose(pieces, (1, 0, 2)).reshape(own_rows, -1).astype(jnp.float32)
    mean_square = jnp.mean(summed * summed, axis=-1, keepdims=True)
    normed = summed * lax.rsqrt(mean_square + norm_eps) * post_gain[None, :]
    return (residual.astype(jnp.float32) + normed).astype(jnp.bfloat16)


def solution(mesh):
    placed = (
        P(("groups", "section"), "head"),
        P(("groups", "section"), "head"),
        P(("groups", "section"), "head"),
        P(("groups", "section", "head"), None),
        P("groups"),
        P("head", "section"),
        P(),
    )
    return jax.shard_map(
        local,
        mesh=mesh,
        in_specs=placed,
        out_specs=P(("groups", "section", "head"), None),
        check_vma=False,
    )
```
